512 devices in a mesh: sx: 16 (over z_lo, y), sy: 32 (over x, z_hi, core).
Axes of the slice: x: 4, y: 8, z: 8 (z_hi: 4, z_lo: 2; z = z_hi * 2 + z_lo), core: 2. Of those that a mesh axis runs over, the one named last changes fastest.
Arguments:
- forward_weights: float32 [4096, 8, 432], P(('sy', 'sx')), may hold values from -6 to 6
- adjoint_weights: float32 [32768, 432], P(('sx', 'sy')), may hold values from -6 to 6
- medium: float32 [4], replicated, may hold values from 0.2 to 0.6
Outputs:
- forward_out: float32 [32768, 432], P(('sx', 'sy'))
- adjoint_out: float32 [8, 4096, 432], P(None, ('sy', 'sx'))
The draws below stay inside these ranges and needn't reach their ends.
All inputs are finite; a program needn't handle non-finite values.
Results may differ from the reference program's by a relative error of at most 0.0003.
Values sent between devices are 32-bit elements; how exact they have to be, the bound alone decides.
No kernel may reach another device: no remote copies, remote signals or barrier semaphores. Data moves between devices by JAX's collectives and lax.ppermute only.
A program may use at most 64 MiB of HBM per device.

```python
import math
import jax
import jax.numpy as jnp
import numpy as np
from jax import lax

ORDER = 6
LEVELS = 4
TGT0 = 8
SHOTS = 1
Q = 216
SRC = 4096
TGT = 32768


def shard_levels(own_key, extent, cuts, smallest, top_value):
    level, own = 1.0, jax.random.fold_in(own_key, 6)
    for position, parts in cuts:
        heights = jnp.exp(jax.random.uniform(jax.random.fold_in(own, position), (parts,), jnp.float32, smallest / len(cuts), top_value / len(cuts)))
        level = level * jnp.repeat(heights, extent[position] // parts).reshape([-1 if axis == position else 1 for axis in range(len(extent))])
    return level


def scatter_about(key, extent, scale, bound, cuts=(), held_as=jnp.bfloat16):
    gain = shard_levels(key, extent, cuts, -0.22, 0.18) if cuts else 1.0
    entries = jax.random.normal(key, extent, jnp.float32) * scale * gain
    return jnp.minimum(jnp.maximum(entries, -bound), bound).astype(held_as)


def setup_inputs(seed: int = 0) -> dict:
    seeds = jax.random.split(jax.random.key(seed), 4)
    forward_weights = scatter_about(seeds[0], (SRC, TGT0, 2 * SHOTS * Q), 1.0, 6.0, ((0, 512),), jnp.float32)
    adjoint_weights = scatter_about(seeds[1], (TGT, 2 * SHOTS * Q), 1.0, 6.0, ((0, 512),), jnp.float32)
    medium = jnp.clip(jax.random.uniform(seeds[2], (4,), jnp.float32, 0.2, 0.6), 0.2, 0.6)
    return {"forward_weights": forward_weights, "adjoint_weights": adjoint_weights, "medium": medium}


two_pi = 2.0 * math.pi
shrink = 1.0 / math.sqrt(8.0)
band = 8.0

def cheb_points(order_count):
    return np.array([(1.0 - math.cos((2 * node_index + 1) * math.pi / (2 * order_count))) / 2.0 for node_index in range(order_count)])

def child_table(order_count):
    nodes_here = cheb_points(order_count)
    halves = []
    for offset_bit in range(2):
        matrix = np.zeros((order_count, order_count))
        for row_index in range(order_count):
            where_at = (nodes_here[row_index] + offset_bit) / 2.0
            for col_index in range(order_count):
                value_now = 1.0
                for other_index in range(order_count):
                    if other_index != col_index:
                        value_now *= (where_at - nodes_here[other_index]) / (nodes_here[col_index] - nodes_here[other_index])
                matrix[row_index, col_index] = value_now
        halves.append(matrix)
    blocks_out = []
    for child_index in range(8):
        along_x = halves[child_index // 4]
        along_y = halves[child_index // 2 % 2]
        along_z = halves[child_index % 2]
        blocks_out.append(np.kron(np.kron(along_x, along_y), along_z))
    return jnp.asarray(np.stack(blocks_out), dtype=jnp.float32)

def box_digits(box_index, groups):
    coord_x = jnp.zeros_like(box_index)
    coord_y = jnp.zeros_like(box_index)
    coord_z = jnp.zeros_like(box_index)
    for group_now in range(groups):
        digit_now = box_index // 8 ** (groups - 1 - group_now) % 8
        coord_x = coord_x * 2 + digit_now // 4
        coord_y = coord_y * 2 + digit_now // 2 % 2
        coord_z = coord_z * 2 + digit_now % 2
    return jnp.stack([coord_x, coord_y, coord_z], axis=-1).astype(jnp.float32)

def box_centres(box_index, groups):
    return (box_digits(box_index, groups) + 0.5) / float(2 ** groups)

def box_points(box_index, groups):
    box_side = band / float(2 ** groups)
    nodes_here = jnp.asarray(cheb_points(ORDER), dtype=jnp.float32)
    grid_x = jnp.repeat(nodes_here, ORDER * ORDER)
    grid_y = jnp.tile(jnp.repeat(nodes_here, ORDER), ORDER)
    grid_z = jnp.tile(nodes_here, ORDER * ORDER)
    offsets = jnp.stack([grid_x, grid_y, grid_z], axis=-1)
    corner = box_digits(box_index, groups)
    return box_side * (corner[..., None, :] + offsets)

def phase_angle(centres, points, medium):
    along = lax.optimization_barrier(jnp.sum(centres * points, axis=-1))
    radius = jnp.sqrt(lax.optimization_barrier(jnp.sum(points * points, axis=-1)))
    travel = medium[0] + lax.optimization_barrier(jnp.sum(medium[1:] * centres, axis=-1))
    return two_pi * (along + travel * radius)

def complex_turn(real_part, imag_part, angle_now, sign_now):
    cosine = jnp.cos(angle_now)
    sine_part = sign_now * jnp.sin(angle_now)
    return (real_part * cosine - imag_part * sine_part, real_part * sine_part + imag_part * cosine)

def forward_level(weights, src_off, tgt_off, level_now, medium, interp):
    src_count, tgt_count = (weights.shape[0], weights.shape[1])
    shot_count, point_count = (weights.shape[3], weights.shape[4])
    parent_count = src_count // 8
    new_targets = tgt_off * 8 + jnp.arange(tgt_count * 8, dtype=jnp.int32)
    centres = box_centres(new_targets, level_now + 2).reshape(tgt_count, 8, 3)
    children = src_off + jnp.arange(src_count, dtype=jnp.int32)
    child_points = box_points(children, LEVELS - level_now).reshape(parent_count, 8, point_count, 3)
    parents = src_off // 8 + jnp.arange(parent_count, dtype=jnp.int32)
    parent_points = box_points(parents, LEVELS - level_now - 1)
    theta_in = phase_angle(centres[None, None, :, :, None, :], child_points[:, :, None, None, :, :], medium)
    theta_out = phase_angle(centres[None, :, :, None, :], parent_points[:, None, None, :, :], medium)
    shaped = weights.reshape(parent_count, 8, tgt_count, 1, 2, shot_count, point_count)
    turned = complex_turn(shaped[:, :, :, :, 0], shaped[:, :, :, :, 1], theta_in[:, :, :, :, None, :], 1.0)
    stacked = jnp.stack(turned, axis=4)
    mixed = jnp.einsum('pctkxhq,cqs->ptkxhs', stacked, interp, precision=lax.Precision.HIGHEST)
    result_re, result_im = complex_turn(mixed[:, :, :, 0], mixed[:, :, :, 1], theta_out[:, :, :, None, :], -1.0)
    output = shrink * jnp.stack([result_re, result_im], axis=3)
    return output.reshape(parent_count, tgt_count * 8, 2, shot_count, point_count)

def adjoint_level(values, tgt_off, src_off, level_now, medium, interp):
    tgt_count, src_count = (values.shape[0], values.shape[1])
    shot_count, point_count = (values.shape[3], values.shape[4])
    parent_count = tgt_count // 8
    targets = tgt_off + jnp.arange(tgt_count, dtype=jnp.int32)
    centres = box_centres(targets, level_now + 2).reshape(parent_count, 8, 3)
    sources = src_off + jnp.arange(src_count, dtype=jnp.int32)
    source_points = box_points(sources, LEVELS - level_now - 1)
    children = src_off * 8 + jnp.arange(src_count * 8, dtype=jnp.int32)
    child_points = box_points(children, LEVELS - level_now).reshape(src_count, 8, point_count, 3)
    theta_out = phase_angle(centres[:, :, None, None, :], source_points[None, None, :, :, :], medium)
    theta_in = phase_angle(centres[:, :, None, None, None, :], child_points[None, None, :, :, :, :], medium)
    shaped = values.reshape(parent_count, 8, src_count, 2, shot_count, point_count)
    turned = complex_turn(shaped[:, :, :, 0], shaped[:, :, :, 1], theta_out[:, :, :, None, :], 1.0)
    stacked = jnp.stack(turned, axis=3)
    spread = jnp.einsum('pkbxhs,cqs->pkbcxhq', stacked, interp, precision=lax.Precision.HIGHEST)
    back_re, back_im = complex_turn(spread[:, :, :, :, 0], spread[:, :, :, :, 1], theta_in[:, :, :, :, None, :], -1.0)
    output = shrink * jnp.stack([lax.optimization_barrier(jnp.sum(back_re, axis=1)), lax.optimization_barrier(jnp.sum(back_im, axis=1))], axis=3)
    return output.reshape(parent_count, src_count * 8, 2, shot_count, point_count)

def blocked(level_fn, array_in):
    first_size, second_size = (array_in.shape[0], array_in.shape[1])
    block_ids = jnp.arange(8, dtype=jnp.int32)
    if first_size >= second_size:
        pieces = array_in.reshape((8, first_size // 8) + array_in.shape[1:])
        results = lax.map(lambda packed: level_fn(packed[0], packed[1] * (first_size // 8), jnp.int32(0)), (pieces, block_ids))
        return results.reshape((results.shape[0] * results.shape[1],) + results.shape[2:])
    pieces = jnp.swapaxes(array_in.reshape((first_size, 8, second_size // 8) + array_in.shape[2:]), 0, 1)
    results = lax.map(lambda packed: level_fn(packed[0], jnp.int32(0), packed[1] * (second_size // 8)), (pieces, block_ids))
    results = jnp.swapaxes(results, 0, 1)
    return results.reshape((results.shape[0], results.shape[1] * results.shape[2]) + results.shape[3:])

def reference(forward_weights, adjoint_weights, medium):
    interp = child_table(ORDER)
    current = forward_weights.reshape(forward_weights.shape[0], forward_weights.shape[1], 2, -1, Q)
    for level_now in range(LEVELS):
        current = blocked(lambda block_now, first_off, second_off: forward_level(block_now, first_off, second_off, level_now, medium, interp), current)
    forward_out = current.reshape(current.shape[1], -1)
    current = adjoint_weights.reshape(adjoint_weights.shape[0], 1, 2, -1, Q)
    for level_now in reversed(range(LEVELS)):
        current = blocked(lambda block_now, first_off, second_off: adjoint_level(block_now, first_off, second_off, level_now, medium, interp), current)
    adjoint_out = current.reshape(current.shape[0], current.shape[1], -1)
    return (forward_out, adjoint_out)
```

```python
import functools
import math

import jax
import jax.numpy as jnp
import numpy as np
from jax import lax
from jax.experimental import pallas as pl
from jax.experimental.pallas import tpu as pltpu
from jax.sharding import PartitionSpec as P

ORDER = 6
Q = 216
W = 256
F32 = jnp.float32
BF16 = jnp.bfloat16
PATTERNS = (7, 6, 5, 4)
KORD = (7, 0, 6, 1, 5, 2, 4, 3)
CUT = 2 * Q - 384
SPILL = Q - 128


def cheb_points():
    return np.array([(1.0 - math.cos((2 * i + 1) * math.pi / (2 * ORDER))) / 2.0 for i in range(ORDER)])


def child_table():
    nodes = cheb_points()
    halves = []
    for bit in range(2):
        matrix = np.zeros((ORDER, ORDER))
        for row in range(ORDER):
            where = (nodes[row] + bit) / 2.0
            for col in range(ORDER):
                value = 1.0
                for other in range(ORDER):
                    if other != col:
                        value *= (where - nodes[other]) / (nodes[col] - nodes[other])
                matrix[row, col] = value
        halves.append(matrix)
    return np.stack(
        [np.kron(np.kron(halves[e // 4], halves[e // 2 % 2]), halves[e % 2]) for e in range(8)]
    )


def tables():
    table = np.zeros((8, W, W))
    table[:, :Q, :Q] = child_table() / math.sqrt(8.0)
    forward = table.reshape(8 * W, W).astype(np.float32)
    halves = []
    for whole in (forward, np.ascontiguousarray(forward.T)):
        high = whole.astype(jnp.bfloat16)
        low = (whole - high.astype(np.float32)).astype(jnp.bfloat16)
        halves.append((high, low))
    nodes = cheb_points()
    grid = np.full((8, W), 0.5)
    grid[0, :Q] = np.repeat(nodes, ORDER * ORDER)
    grid[1, :Q] = np.tile(np.repeat(nodes, ORDER), ORDER)
    grid[2, :Q] = np.tile(nodes, ORDER * ORDER)
    return halves, grid.astype(np.float32)


def turn_polynomials():
    x = (np.cos(np.pi * (np.arange(400) + 0.5) / 400) + 1.0) / 8.0
    f = np.sqrt(x)
    s = np.polynomial.chebyshev.Chebyshev.fit(x, np.sin(2 * np.pi * f) / f, 5, domain=[0, 0.25])
    c = np.polynomial.chebyshev.Chebyshev.fit(x, np.cos(2 * np.pi * f), 6, domain=[0, 0.25])
    return [
        [float(v) for v in p.convert(kind=np.polynomial.Polynomial).coef] for p in (s, c)
    ]


SIN, COS = turn_polynomials()


def horner(coefs, z):
    value = jnp.full_like(z, coefs[-1])
    for c in coefs[-2::-1]:
        value = value * z + c
    return value


def cis(turns):
    f = turns - jnp.round(turns)
    z = f * f
    return horner(COS, z), f * horner(SIN, z)


def digit_coords(index, digits):
    out = []
    for bit in (2, 1, 0):
        value = None
        for d in range(digits):
            part = (index >> (3 * d + bit)) & 1
            part = part << d if d else part
            value = part if value is None else value + part
        out.append(value)
    return out


def as_f32(values):
    return [v.astype(F32) for v in values]


def rows8():
    return lax.broadcasted_iota(jnp.int32, (8, W), 0)


def travel_rays(corner, side, grid_ref, med):
    p = [side * (corner[d] + grid_ref[d : d + 1, :]) for d in range(3)]
    r = jnp.sqrt(p[0] * p[0] + p[1] * p[1] + p[2] * p[2])
    return r, [p[d] + med[d + 1] * r for d in range(3)]


def patterns(level, rays):
    step = 1.0 / 2 ** (level + 3)
    x, y, z = (step * v for v in rays)
    a, b = x + y, x - y
    return [cis(a + z), cis(a - z), cis(b + z), cis(b - z)]


def pick(table, row):
    return [(c[row : row + 1, :], s[row : row + 1, :]) for c, s in table]


def split16(first, second):
    whole = jnp.concatenate([first, second], axis=0)
    high = whole.astype(BF16)
    return high, (whole - high.astype(F32)).astype(BF16)


def forward_put(xs_ref, e, re, im, turn):
    cols = slice(e * W, (e + 1) * W)
    for s, (c, sn) in enumerate(turn):
        a, b, d, g = re * c, im * sn, im * c, re * sn
        for base, one, two in ((0, a - b, a + b), (64, d + g, d - g)):
            high, low = split16(one, two)
            row = base + 16 * s
            xs_ref[row : row + 16, cols] = high
            xs_ref[128 + row : 144 + row, cols] = low


def product(x, xh, wh, wl):
    both = jnp.dot(x, wh, preferred_element_type=F32)
    return both[:128] + both[128:] + jnp.dot(xh, wl, preferred_element_type=F32)


def forward_product(xs_ref, wh_ref, wl_ref):
    return product(xs_ref[...], xs_ref[0:128, :], wh_ref[...], wl_ref[...])


def adjoint_put(xs_ref, k, first, second):
    for base, one, two in ((0, first[0], second[0]), (64, first[1], second[1])):
        high, low = split16(one, two)
        row = base + 8 * k
        xs_ref[row : row + 16, :] = high
        xs_ref[128 + row : 144 + row, :] = low


def adjoint_child(xs_ref, wh_ref, wl_ref, e, turn):
    cols = slice(e * W, (e + 1) * W)
    y = product(xs_ref[...], xs_ref[0:128, :], wh_ref[:, cols], wl_ref[:, cols])
    re = im = None
    for k, (c, sn) in zip(PATTERNS, turn):
        o = 7 - k
        kr, ki = y[8 * k : 8 * k + 8], y[64 + 8 * k : 72 + 8 * k]
        br, bi = y[8 * o : 8 * o + 8], y[64 + 8 * o : 72 + 8 * o]
        one = c * (kr + br) + sn * (ki - bi)
        two = c * (ki + bi) - sn * (kr - br)
        re, im = (one, two) if re is None else (re + one, im + two)
    return re, im


def quarters(re, im):
    return re[:, :128], re[:, 128:], im[:, :128], im[:, 128:]


def join(a, b):
    return jnp.concatenate([a, b], axis=1)


def unpack(x_ref, tail_ref):
    tail_ref[...] = jnp.zeros_like(tail_ref)
    tail_ref[:, 0:CUT] = x_ref[:, 384 : 2 * Q]
    lane = lax.broadcasted_iota(jnp.int32, (64, 128), 1)
    x0, x1, x2, x3 = x_ref[:, 0:128], x_ref[:, 128:256], x_ref[:, 256:384], tail_ref[...]
    shift = 128 - SPILL
    r1, r2, r3 = (pltpu.roll(v, shift, 1) for v in (x1, x2, x3))
    re = join(x0, jnp.where(lane < SPILL, x1, 0.0))
    im = join(
        jnp.where(lane < shift, r1, r2),
        jnp.where(lane < shift, r2, jnp.where(lane < SPILL, r3, 0.0)),
    )
    return re, im


def pack(parts, out_ref):
    r0, r1, i0, i1 = (parts[64 * c : 64 * c + 64, :] for c in range(4))
    lane = lax.broadcasted_iota(jnp.int32, (64, 128), 1)
    s0, s1 = pltpu.roll(i0, SPILL, 1), pltpu.roll(i1, SPILL, 1)
    out_ref[:, 0:128] = r0
    out_ref[:, 128:256] = jnp.where(lane < SPILL, r1, s0)
    out_ref[:, 256:384] = jnp.where(lane < SPILL, s0, s1)
    out_ref[:, 384 : 2 * Q] = s1[:, 0:CUT]


def medium_of(med_ref):
    return [med_ref[i] for i in range(4)]


def own_source(extra_rows):
    own = lax.axis_index("sy") * 16 + lax.axis_index("sx")
    high = digit_coords(own, 3)
    low = digit_coords(extra_rows, 1)
    return as_f32([low[d] + 2 * high[d] for d in range(3)])


def root_turn(med, corner, rays0):
    r, rays = rays0
    centre = [(v + 0.5) * 0.5 for v in corner]
    travel = med[0] * r
    return cis(travel + centre[0] * rays[0] + centre[1] * rays[1] + centre[2] * rays[2])


def end_turn(med, block, across, grid_ref):
    own = lax.axis_index("sx") * 32 + lax.axis_index("sy")
    high = digit_coords(own, 3)
    row = digit_coords(rows8(), 1)
    fixed = digit_coords(block, 1)
    wr, wf = (1, 2) if across else (2, 1)
    centre = [
        ((4 * high[d] + wf * fixed[d] + wr * row[d]).astype(F32) + 0.5) * (1.0 / 32.0)
        for d in range(3)
    ]
    p = [8.0 * grid_ref[d : d + 1, :] for d in range(3)]
    r = jnp.sqrt(p[0] * p[0] + p[1] * p[1] + p[2] * p[2])
    u = med[0] * r
    for d in range(3):
        u = u + centre[d] * (p[d] + med[d + 1] * r)
    return cis(u)


def level_patterns(level, corner, side, grid_ref, med):
    return patterns(level, travel_rays(corner, side, grid_ref, med)[1])


def level1_tables(grid_ref, med):
    high = digit_coords(lax.axis_index("sy") * 2, 2)
    first = digit_coords(rows8(), 1)
    out = []
    for half in range(2):
        mid = digit_coords(lax.axis_index("sy") * 2 + half, 2)
        corner = as_f32([first[d] + 2 * mid[d] for d in range(3)])
        out.append(level_patterns(1, corner, 1.0, grid_ref, med))
    return out


def level1_turn(both, e):
    upper = rows8() < 4
    return [
        (
            jnp.where(upper, c0[e : e + 1, :], c1[e : e + 1, :]),
            jnp.where(upper, s0[e : e + 1, :], s1[e : e + 1, :]),
        )
        for (c0, s0), (c1, s1) in zip(*both)
    ]


def level2_turn(e, grid_ref, med):
    parent = digit_coords(rows8(), 1)
    child = digit_coords(e, 1)
    corner = as_f32([2 * parent[d] + child[d] for d in range(3)])
    return level_patterns(2, corner, 2.0, grid_ref, med)


def level3_table(grid_ref, med):
    return level_patterns(3, as_f32(digit_coords(rows8(), 1)), 4.0, grid_ref, med)


def rows_of(ref, start, stride, count=8):
    return ref[pl.ds(start, count, stride=stride), :]


def wide(ref, start, stride):
    return join(rows_of(ref, start[0], stride), rows_of(ref, start[1], stride)), join(
        rows_of(ref, start[2], stride), rows_of(ref, start[3], stride)
    )


def forward0(med_ref, grid_ref, x_ref, wh_ref, wl_ref, out_ref, xs_ref, tail_ref):
    med = medium_of(med_ref)
    r, rays = travel_rays(own_source(rows8()), 0.5, grid_ref, med)
    table = patterns(0, rays)
    target = as_f32(digit_coords(rows8(), 1))
    re, im = unpack(x_ref, tail_ref)
    for e in range(8):
        one = slice(e, e + 1)
        c, s = root_turn(med, target, (r[one], [v[one] for v in rays]))
        xr, xi = re[8 * e : 8 * e + 8], im[8 * e : 8 * e + 8]
        forward_put(xs_ref, e, xr * c - xi * s, xr * s + xi * c, pick(table, e))
    y = forward_product(xs_ref, wh_ref, wl_ref)
    for pos, k in enumerate(KORD):
        four = quarters(y[8 * pos : 8 * pos + 8], y[64 + 8 * pos : 72 + 8 * pos])
        for c, v in enumerate(four):
            out_ref[pl.ds((k >> 2) * 16 + c * 4 + (k & 3), 8, stride=32), :] = v


def forward1(chunk, med_ref, grid_ref, x_ref, wh_ref, wl_ref, *rest):
    if chunk == 16:
        other_ref, out_ref, xs_ref = rest
        for dest in range(32):
            out_ref[dest * 16 + 8 : dest * 16 + 16, :] = other_ref[dest * 8 : dest * 8 + 8, :]
    else:
        out_ref, xs_ref = rest
    med = medium_of(med_ref)
    both = level1_tables(grid_ref, med)
    upper = lax.broadcasted_iota(jnp.int32, (8, 128), 0) < 4
    for e in range(8):
        halves = []
        for part in range(2):
            t0 = x_ref[e * 16 + 8 * part : e * 16 + 8 * part + 8, :]
            t1 = x_ref[128 + e * 16 + 8 * part : 128 + e * 16 + 8 * part + 8, :]
            halves.append(
                join(
                    jnp.where(upper, t0, pltpu.roll(t1, 4, 0)),
                    jnp.where(upper, pltpu.roll(t0, 4, 0), t1),
                )
            )
        forward_put(xs_ref, e, halves[0], halves[1], level1_turn(both, e))
    y = forward_product(xs_ref, wh_ref, wl_ref)
    for pos, k in enumerate(KORD):
        four = quarters(y[8 * pos : 8 * pos + 8], y[64 + 8 * pos : 72 + 8 * pos])
        for c, v in enumerate(four):
            for p in range(2):
                start = k * chunk + p * 4 + c
                out_ref[pl.ds(start, 4, stride=8 * chunk), :] = v[4 * p : 4 * p + 4]


def forward23(chunk, med_ref, grid_ref, x_ref, wh_ref, wl_ref, out_ref, xs_ref, mid_ref):
    med = medium_of(med_ref)
    for e in range(8):
        base = (e >> 1) * chunk + (e & 1) * 4
        re, im = wide(x_ref, [base + c for c in range(4)], 4 * chunk)
        forward_put(xs_ref, e, re, im, level2_turn(e, grid_ref, med))
    y = forward_product(xs_ref, wh_ref, wl_ref)
    for pos, k in enumerate(KORD):
        four = quarters(y[8 * pos : 8 * pos + 8], y[64 + 8 * pos : 72 + 8 * pos])
        for c, v in enumerate(four):
            mid_ref[64 * c + 8 * k : 64 * c + 8 * k + 8, :] = v
    table = level3_table(grid_ref, med)
    for e in range(8):
        re, im = wide(mid_ref, [64 * c + e for c in range(4)], 8)
        forward_put(xs_ref, e, re, im, pick(table, e))
    y = forward_product(xs_ref, wh_ref, wl_ref)
    for pos, k in enumerate(KORD):
        c, s = end_turn(med, k, False, grid_ref)
        re, im = y[8 * pos : 8 * pos + 8], y[64 + 8 * pos : 72 + 8 * pos]
        four = quarters(re * c + im * s, im * c - re * s)
        for q, v in enumerate(four):
            mid_ref[pl.ds(64 * q + k, 8, stride=8), :] = v
    pack(mid_ref, out_ref)


def adjoint32(med_ref, grid_ref, x_ref, wh_ref, wl_ref, out_ref, xs_ref, mid_ref, tail_ref):
    med = medium_of(med_ref)
    re, im = unpack(x_ref, tail_ref)
    for k in range(8):
        c, s = end_turn(med, k, True, grid_ref)
        xr, xi = re[8 * k : 8 * k + 8], im[8 * k : 8 * k + 8]
        for q, v in enumerate(quarters(xr * c - xi * s, xr * s + xi * c)):
            mid_ref[64 * q + 8 * k : 64 * q + 8 * k + 8, :] = v
    for k in range(0, 8, 2):
        adjoint_put(
            xs_ref,
            k,
            wide(mid_ref, [64 * c + k for c in range(4)], 8),
            wide(mid_ref, [64 * c + k + 1 for c in range(4)], 8),
        )
    table = level3_table(grid_ref, med)
    for e in range(8):
        re, im = adjoint_child(xs_ref, wh_ref, wl_ref, e, pick(table, e))
        for q, v in enumerate(quarters(re, im)):
            mid_ref[pl.ds(64 * q + e, 8, stride=8), :] = v
    for k in range(0, 8, 2):
        pair = []
        for j in (k, k + 1):
            r0, r1, i0, i1 = (mid_ref[64 * c + 8 * j : 64 * c + 8 * j + 8, :] for c in range(4))
            pair.append((join(r0, r1), join(i0, i1)))
        adjoint_put(xs_ref, k, pair[0], pair[1])
    for e in range(8):
        re, im = adjoint_child(xs_ref, wh_ref, wl_ref, e, level2_turn(e, grid_ref, med))
        for q, v in enumerate(quarters(re, im)):
            out_ref[pl.ds((e >> 1) * 8 + (e & 1) * 4 + q, 8, stride=32), :] = v


def adjoint1(chunk, med_ref, grid_ref, x_ref, wh_ref, wl_ref, out_ref, xs_ref):
    med = medium_of(med_ref)
    both = level1_tables(grid_ref, med)
    for k in range(0, 8, 2):
        pair = []
        for j in (k, k + 1):
            four = []
            for c in range(4):
                start = j * chunk + (chunk - 8) + c
                four.append(
                    jnp.concatenate(
                        [rows_of(x_ref, start + 4 * p, 8 * chunk, 4) for p in range(2)], axis=0
                    )
                )
            pair.append((join(four[0], four[1]), join(four[2], four[3])))
        adjoint_put(xs_ref, k, pair[0], pair[1])
    for e in range(8):
        re, im = adjoint_child(xs_ref, wh_ref, wl_ref, e, level1_turn(both, e))
        for q, v in enumerate(quarters(re, im)):
            for p in range(2):
                start = (8 * p + e) * 16 + 4 * q
                out_ref[start : start + 4, :] = v[4 * p : 4 * p + 4]


def adjoint0(med_ref, grid_ref, x_ref, wh_ref, wl_ref, out_ref, xs_ref, mid_ref):
    med = medium_of(med_ref)
    r, rays = travel_rays(own_source(rows8()), 0.5, grid_ref, med)
    table = patterns(0, rays)
    target = as_f32(digit_coords(rows8(), 1))
    for k in range(0, 8, 2):
        pair = [
            wide(x_ref, [(j >> 2) * 16 + c * 4 + (j & 3) for c in range(4)], 32)
            for j in (k, k + 1)
        ]
        adjoint_put(xs_ref, k, pair[0], pair[1])
    for e in range(8):
        re, im = adjoint_child(xs_ref, wh_ref, wl_ref, e, pick(table, e))
        one = slice(e, e + 1)
        c, s = root_turn(med, target, (r[one], [v[one] for v in rays]))
        for q, v in enumerate(quarters(re * c + im * s, im * c - re * s)):
            mid_ref[pl.ds(64 * q + e, 8, stride=8), :] = v
    pack(mid_ref, out_ref)


def call(kernel, name, out_shape, scratch, levels, *operands):
    vmem = pl.BlockSpec(memory_space=pltpu.VMEM)
    return pl.pallas_call(
        kernel,
        out_shape=jax.ShapeDtypeStruct(out_shape, F32),
        in_specs=[pl.BlockSpec(memory_space=pltpu.SMEM)] + [vmem] * (len(operands) - 1),
        out_specs=vmem,
        scratch_shapes=scratch,
        compiler_params=pltpu.CompilerParams(vmem_limit_bytes=24 * 2**20),
        cost_estimate=pl.CostEstimate(
            flops=levels * 10**9, bytes_accessed=2 * 10**6, transcendentals=0
        ),
        name=name,
    )(*operands)


CHUNK = 16


def shards(forward_weights, adjoint_weights, medium):
    ((fh, fl), (ah, al)), grid = tables()
    fh, fl, ah, al, grid = (jnp.asarray(v) for v in (fh, fl, ah, al, grid))
    fscr = pltpu.VMEM((256, 8 * W), BF16)
    ascr = pltpu.VMEM((256, W), BF16)
    mid = pltpu.VMEM((256, 128), F32)
    tail = pltpu.VMEM((64, 128), F32)
    swap = functools.partial(lax.all_to_all, split_axis=0, concat_axis=0, tiled=True)

    def over(x, axis, count):
        shape = x.shape
        return swap(x.reshape(count, shape[0] // count, 128), axis).reshape(shape)

    fw = forward_weights.reshape(64, 2 * Q)
    f0 = call(forward0, "forward0", (256, 128), [fscr, tail], 1, medium, grid, fw, fh, fl)
    f0 = over(f0, "sx", 16)
    a2 = call(
        adjoint32, "adjoint32", (256, 128), [ascr, mid, tail], 2, medium, grid, adjoint_weights, ah, al
    )
    f1 = functools.partial(forward1, CHUNK)
    both = call(f1, "forward1", (512, 128), [fscr], 1, medium, grid, f0, fh, fl, a2)
    both = over(both, "sy", 32)
    a1 = functools.partial(adjoint1, CHUNK)
    a1 = call(a1, "adjoint1", (256, 128), [ascr], 1, medium, grid, both, ah, al)
    a1 = over(a1, "sx", 16)
    f3 = functools.partial(forward23, CHUNK)
    f3 = call(f3, "forward23", (64, 2 * Q), [fscr, mid], 2, medium, grid, both, fh, fl)
    a0 = call(adjoint0, "adjoint0", (64, 2 * Q), [ascr, mid], 1, medium, grid, a1, ah, al)
    return f3, a0.reshape(8, 8, 2 * Q)


def solution(mesh):
    return jax.shard_map(
        shards,
        mesh=mesh,
        in_specs=(P(("sy", "sx"), None, None), P(("sx", "sy"), None), P()),
        out_specs=(P(("sx", "sy"), None), P(None, ("sy", "sx"), None)),
        check_vma=False,
    )
```

```python
import functools
import math

import jax
import jax.numpy as jnp
import numpy as np
from jax import lax
from jax.experimental import pallas as pl
from jax.experimental.pallas import tpu as pltpu
from jax.sharding import PartitionSpec as P

ORDER = 6
Q = 216
W = 256
F32 = jnp.float32
BF16 = jnp.bfloat16
PATTERNS = (7, 6, 5, 4)
KORD = (7, 0, 6, 1, 5, 2, 4, 3)
PIECES = 4
CUT = 2 * Q - 384
SPILL = Q - 128


def cheb_points():
    return np.array([(1.0 - math.cos((2 * i + 1) * math.pi / (2 * ORDER))) / 2.0 for i in range(ORDER)])


def child_table():
    nodes = cheb_points()
    halves = []
    for bit in range(2):
        matrix = np.zeros((ORDER, ORDER))
        for row in range(ORDER):
            where = (nodes[row] + bit) / 2.0
            for col in range(ORDER):
                value = 1.0
                for other in range(ORDER):
                    if other != col:
                        value *= (where - nodes[other]) / (nodes[col] - nodes[other])
                matrix[row, col] = value
        halves.append(matrix)
    return np.stack(
        [np.kron(np.kron(halves[e // 4], halves[e // 2 % 2]), halves[e % 2]) for e in range(8)]
    )


def tables():
    table = np.zeros((8, W, W))
    table[:, :Q, :Q] = child_table() / math.sqrt(8.0)
    whole = table.reshape(8 * W, W).astype(np.float32)
    high = whole.astype(jnp.bfloat16)
    return high, (whole - high.astype(np.float32)).astype(jnp.bfloat16)


def turn_polynomials():
    x = (np.cos(np.pi * (np.arange(400) + 0.5) / 400) + 1.0) / 8.0
    f = np.sqrt(x)
    s = np.polynomial.chebyshev.Chebyshev.fit(x, np.sin(2 * np.pi * f) / f, 5, domain=[0, 0.25])
    c = np.polynomial.chebyshev.Chebyshev.fit(x, np.cos(2 * np.pi * f), 6, domain=[0, 0.25])
    return [
        [float(v) for v in p.convert(kind=np.polynomial.Polynomial).coef] for p in (s, c)
    ]


SIN, COS = turn_polynomials()


def horner(coefs, z):
    value = jnp.full_like(z, coefs[-1])
    for c in coefs[-2::-1]:
        value = value * z + c
    return value


def cis(turns):
    f = turns - jnp.round(turns)
    z = f * f
    return horner(COS, z), f * horner(SIN, z)


def digit_coords(index, digits):
    out = []
    for bit in (2, 1, 0):
        value = None
        for d in range(digits):
            part = (index >> (3 * d + bit)) & 1
            part = part << d if d else part
            value = part if value is None else value + part
        out.append(value)
    return out


def as_f32(values):
    return [v.astype(F32) for v in values]


def rows8():
    return lax.broadcasted_iota(jnp.int32, (8, W), 0)


def grid_points():
    t = lax.broadcasted_iota(jnp.int32, (8, W), 1)
    i = (t * 7282) >> 18
    ij = (t * 10923) >> 16
    nodes = [float(v) for v in cheb_points()]
    out = []
    for n in (i, ij - 6 * i, t - 6 * ij):
        value = jnp.full((8, W), nodes[5], F32)
        for m in range(4, -1, -1):
            value = jnp.where(n == m, nodes[m], value)
        out.append(value)
    return out


def travel_rays(corner, side, grid, med):
    p = [side * (corner[d] + grid[d]) for d in range(3)]
    r = jnp.sqrt(p[0] * p[0] + p[1] * p[1] + p[2] * p[2])
    return r, [p[d] + med[d + 1] * r for d in range(3)]


def patterns(level, rays):
    step = 1.0 / 2 ** (level + 3)
    x, y, z = (step * v for v in rays)
    a, b = x + y, x - y
    return [cis(a + z), cis(a - z), cis(b + z), cis(b - z)]


def pick(table, row):
    return [(c[row : row + 1, :], s[row : row + 1, :]) for c, s in table]


def split16(first, second):
    whole = jnp.concatenate([first, second], axis=0)
    high = whole.astype(BF16)
    return high, (whole - high.astype(F32)).astype(BF16)


def forward_put(xs_ref, e, re, im, turn):
    cols = slice(e * W, (e + 1) * W)
    for s, (c, sn) in enumerate(turn):
        a, b, d, g = re * c, im * sn, im * c, re * sn
        for base, one, two in ((0, a - b, a + b), (64, d + g, d - g)):
            high, low = split16(one, two)
            row = base + 16 * s
            xs_ref[row : row + 16, cols] = high
            xs_ref[128 + row : 144 + row, cols] = low


def product(x, xh, wh, wl, side):
    dot = functools.partial(
        lax.dot_general, dimension_numbers=(((1,), (side,)), ((), ())), preferred_element_type=F32
    )
    both = dot(x, wh)
    return both[:128] + both[128:] + dot(xh, wl)


def forward_product(xs_ref, wh_ref, wl_ref):
    return product(xs_ref[...], xs_ref[0:128, :], wh_ref[...], wl_ref[...], 0)


def adjoint_put(xs_ref, k, first, second):
    for base, one, two in ((0, first[0], second[0]), (64, first[1], second[1])):
        high, low = split16(one, two)
        row = base + 8 * k
        xs_ref[row : row + 16, :] = high
        xs_ref[128 + row : 144 + row, :] = low


def adjoint_child(xs_ref, wh_ref, wl_ref, e, turn):
    cols = slice(e * W, (e + 1) * W)
    y = product(xs_ref[...], xs_ref[0:128, :], wh_ref[cols, :], wl_ref[cols, :], 1)
    re = im = None
    for k, (c, sn) in zip(PATTERNS, turn):
        o = 7 - k
        kr, ki = y[8 * k : 8 * k + 8], y[64 + 8 * k : 72 + 8 * k]
        br, bi = y[8 * o : 8 * o + 8], y[64 + 8 * o : 72 + 8 * o]
        one = c * (kr + br) + sn * (ki - bi)
        two = c * (ki + bi) - sn * (kr - br)
        re, im = (one, two) if re is None else (re + one, im + two)
    return re, im


def quarters(re, im):
    return re[:, :128], re[:, 128:], im[:, :128], im[:, 128:]


def join(a, b):
    return jnp.concatenate([a, b], axis=1)


def unpack(x_ref, tail_ref):
    tail_ref[...] = jnp.zeros_like(tail_ref)
    tail_ref[:, 0:CUT] = x_ref[:, 384 : 2 * Q]
    lane = lax.broadcasted_iota(jnp.int32, (64, 128), 1)
    x0, x1, x2, x3 = x_ref[:, 0:128], x_ref[:, 128:256], x_ref[:, 256:384], tail_ref[...]
    shift = 128 - SPILL
    r1, r2, r3 = (pltpu.roll(v, shift, 1) for v in (x1, x2, x3))
    re = join(x0, jnp.where(lane < SPILL, x1, 0.0))
    im = join(
        jnp.where(lane < shift, r1, r2),
        jnp.where(lane < shift, r2, jnp.where(lane < SPILL, r3, 0.0)),
    )
    return re, im


def pack(parts, out_ref):
    r0, r1, i0, i1 = (parts[64 * c : 64 * c + 64, :] for c in range(4))
    lane = lax.broadcasted_iota(jnp.int32, (64, 128), 1)
    s0, s1 = pltpu.roll(i0, SPILL, 1), pltpu.roll(i1, SPILL, 1)
    out_ref[:, 0:128] = r0
    out_ref[:, 128:256] = jnp.where(lane < SPILL, r1, s0)
    out_ref[:, 256:384] = jnp.where(lane < SPILL, s0, s1)
    out_ref[:, 384 : 2 * Q] = s1[:, 0:CUT]


def medium_of(med_ref):
    return [jnp.broadcast_to(med_ref[0:1, i : i + 1], (8, W)) for i in range(4)]


def own_source(extra_rows):
    own = lax.axis_index("sy") * 16 + lax.axis_index("sx")
    high = digit_coords(own, 3)
    low = digit_coords(extra_rows, 1)
    return as_f32([low[d] + 2 * high[d] for d in range(3)])


def root_turn(med, corner, rays0):
    r, rays = rays0
    centre = [(v + 0.5) * 0.5 for v in corner]
    travel = med[0] * r
    return cis(travel + centre[0] * rays[0] + centre[1] * rays[1] + centre[2] * rays[2])


def end_turn(med, block, across, grid):
    own = lax.axis_index("sx") * 32 + lax.axis_index("sy")
    high = digit_coords(own, 3)
    row = digit_coords(rows8(), 1)
    fixed = digit_coords(block, 1)
    wr, wf = (1, 2) if across else (2, 1)
    centre = [
        ((4 * high[d] + wf * fixed[d] + wr * row[d]).astype(F32) + 0.5) * (1.0 / 32.0)
        for d in range(3)
    ]
    p = [8.0 * grid[d] for d in range(3)]
    r = jnp.sqrt(p[0] * p[0] + p[1] * p[1] + p[2] * p[2])
    u = med[0] * r
    for d in range(3):
        u = u + centre[d] * (p[d] + med[d + 1] * r)
    return cis(u)


def level_patterns(level, corner, side, grid, med):
    return patterns(level, travel_rays(corner, side, grid, med)[1])


def level1_tables(grid, med):
    high = digit_coords(lax.axis_index("sy") * 2, 2)
    first = digit_coords(rows8(), 1)
    out = []
    for half in range(2):
        mid = digit_coords(lax.axis_index("sy") * 2 + half, 2)
        corner = as_f32([first[d] + 2 * mid[d] for d in range(3)])
        out.append(level_patterns(1, corner, 1.0, grid, med))
    return out


def level1_turn(both, e):
    upper = rows8() < 4
    return [
        (
            jnp.where(upper, c0[e : e + 1, :], c1[e : e + 1, :]),
            jnp.where(upper, s0[e : e + 1, :], s1[e : e + 1, :]),
        )
        for (c0, s0), (c1, s1) in zip(*both)
    ]


def level2_turn(e, grid, med):
    parent = digit_coords(rows8(), 1)
    child = digit_coords(e, 1)
    corner = as_f32([2 * parent[d] + child[d] for d in range(3)])
    return level_patterns(2, corner, 2.0, grid, med)


def level3_table(grid, med):
    return level_patterns(3, as_f32(digit_coords(rows8(), 1)), 4.0, grid, med)


def rows_of(ref, start, stride, count=8):
    return ref[pl.ds(start, count, stride=stride), :]


def wide(ref, start, stride):
    return join(rows_of(ref, start[0], stride), rows_of(ref, start[1], stride)), join(
        rows_of(ref, start[2], stride), rows_of(ref, start[3], stride)
    )


def forward0(med_hbm, x_hbm, wh_hbm, wl_hbm, out_ref, xs_ref, tail_ref, med_ref, x_ref, wh_ref, wl_ref, sems):
    copies = [
        pltpu.make_async_copy(med_hbm, med_ref, sems.at[0]),
        pltpu.make_async_copy(x_hbm, x_ref, sems.at[1]),
    ]
    step = 8 * W // PIECES
    for i, (src, dst) in enumerate(((wh_hbm, wh_ref), (wl_hbm, wl_ref))):
        for j in range(PIECES):
            part = pl.ds(step * j, step)
            copies.append(
                pltpu.make_async_copy(src.at[part, :], dst.at[part, :], sems.at[2 + PIECES * i + j])
            )
    for copy in copies:
        copy.start()
    copies[0].wait()
    med, grid = medium_of(med_ref), grid_points()
    r, rays = travel_rays(own_source(rows8()), 0.5, grid, med)
    table = patterns(0, rays)
    target = as_f32(digit_coords(rows8(), 1))
    copies[1].wait()
    re, im = unpack(x_ref, tail_ref)
    for e in range(8):
        one = slice(e, e + 1)
        c, s = root_turn(med, target, (r[one], [v[one] for v in rays]))
        xr, xi = re[8 * e : 8 * e + 8], im[8 * e : 8 * e + 8]
        forward_put(xs_ref, e, xr * c - xi * s, xr * s + xi * c, pick(table, e))
    for copy in copies[2:]:
        copy.wait()
    y = forward_product(xs_ref, wh_ref, wl_ref)
    for pos, k in enumerate(KORD):
        four = quarters(y[8 * pos : 8 * pos + 8], y[64 + 8 * pos : 72 + 8 * pos])
        for c, v in enumerate(four):
            out_ref[pl.ds((k >> 2) * 16 + c * 4 + (k & 3), 8, stride=32), :] = v


def forward1(chunk, med_ref, x_ref, wh_ref, wl_ref, *rest):
    if chunk == 16:
        other_ref, out_ref, xs_ref = rest
        for dest in range(32):
            out_ref[dest * 16 + 8 : dest * 16 + 16, :] = other_ref[dest * 8 : dest * 8 + 8, :]
    else:
        out_ref, xs_ref = rest
    med, grid = medium_of(med_ref), grid_points()
    both = level1_tables(grid, med)
    upper = lax.broadcasted_iota(jnp.int32, (8, 128), 0) < 4
    for e in range(8):
        halves = []
        for part in range(2):
            t0 = x_ref[e * 16 + 8 * part : e * 16 + 8 * part + 8, :]
            t1 = x_ref[128 + e * 16 + 8 * part : 128 + e * 16 + 8 * part + 8, :]
            halves.append(
                join(
                    jnp.where(upper, t0, pltpu.roll(t1, 4, 0)),
                    jnp.where(upper, pltpu.roll(t0, 4, 0), t1),
                )
            )
        forward_put(xs_ref, e, halves[0], halves[1], level1_turn(both, e))
    y = forward_product(xs_ref, wh_ref, wl_ref)
    for pos, k in enumerate(KORD):
        four = quarters(y[8 * pos : 8 * pos + 8], y[64 + 8 * pos : 72 + 8 * pos])
        for c, v in enumerate(four):
            for p in range(2):
                start = k * chunk + p * 4 + c
                out_ref[pl.ds(start, 4, stride=8 * chunk), :] = v[4 * p : 4 * p + 4]


def forward23(chunk, med_ref, x_ref, wh_ref, wl_ref, out_ref, xs_ref, mid_ref):
    med, grid = medium_of(med_ref), grid_points()
    for e in range(8):
        base = (e >> 1) * chunk + (e & 1) * 4
        re, im = wide(x_ref, [base + c for c in range(4)], 4 * chunk)
        forward_put(xs_ref, e, re, im, level2_turn(e, grid, med))
    y = forward_product(xs_ref, wh_ref, wl_ref)
    for pos, k in enumerate(KORD):
        four = quarters(y[8 * pos : 8 * pos + 8], y[64 + 8 * pos : 72 + 8 * pos])
        for c, v in enumerate(four):
            mid_ref[64 * c + 8 * k : 64 * c + 8 * k + 8, :] = v
    table = level3_table(grid, med)
    for e in range(8):
        re, im = wide(mid_ref, [64 * c + e for c in range(4)], 8)
        forward_put(xs_ref, e, re, im, pick(table, e))
    y = forward_product(xs_ref, wh_ref, wl_ref)
    for pos, k in enumerate(KORD):
        c, s = end_turn(med, k, False, grid)
        re, im = y[8 * pos : 8 * pos + 8], y[64 + 8 * pos : 72 + 8 * pos]
        four = quarters(re * c + im * s, im * c - re * s)
        for q, v in enumerate(four):
            mid_ref[pl.ds(64 * q + k, 8, stride=8), :] = v
    pack(mid_ref, out_ref)


def adjoint32(med_ref, x_ref, wh_ref, wl_ref, out_ref, xs_ref, mid_ref, tail_ref):
    med, grid = medium_of(med_ref), grid_points()
    re, im = unpack(x_ref, tail_ref)
    for k in range(8):
        c, s = end_turn(med, k, True, grid)
        xr, xi = re[8 * k : 8 * k + 8], im[8 * k : 8 * k + 8]
        for q, v in enumerate(quarters(xr * c - xi * s, xr * s + xi * c)):
            mid_ref[64 * q + 8 * k : 64 * q + 8 * k + 8, :] = v
    for k in range(0, 8, 2):
        adjoint_put(
            xs_ref,
            k,
            wide(mid_ref, [64 * c + k for c in range(4)], 8),
            wide(mid_ref, [64 * c + k + 1 for c in range(4)], 8),
        )
    table = level3_table(grid, med)
    for e in range(8):
        re, im = adjoint_child(xs_ref, wh_ref, wl_ref, e, pick(table, e))
        for q, v in enumerate(quarters(re, im)):
            mid_ref[pl.ds(64 * q + e, 8, stride=8), :] = v
    for k in range(0, 8, 2):
        pair = []
        for j in (k, k + 1):
            r0, r1, i0, i1 = (mid_ref[64 * c + 8 * j : 64 * c + 8 * j + 8, :] for c in range(4))
            pair.append((join(r0, r1), join(i0, i1)))
        adjoint_put(xs_ref, k, pair[0], pair[1])
    for e in range(8):
        re, im = adjoint_child(xs_ref, wh_ref, wl_ref, e, level2_turn(e, grid, med))
        for q, v in enumerate(quarters(re, im)):
            out_ref[pl.ds((e >> 1) * 8 + (e & 1) * 4 + q, 8, stride=32), :] = v


def adjoint1(chunk, med_ref, x_ref, wh_ref, wl_ref, out_ref, xs_ref):
    med, grid = medium_of(med_ref), grid_points()
    both = level1_tables(grid, med)
    for k in range(0, 8, 2):
        pair = []
        for j in (k, k + 1):
            four = []
            for c in range(4):
                start = j * chunk + (chunk - 8) + c
                four.append(
                    jnp.concatenate(
                        [rows_of(x_ref, start + 4 * p, 8 * chunk, 4) for p in range(2)], axis=0
                    )
                )
            pair.append((join(four[0], four[1]), join(four[2], four[3])))
        adjoint_put(xs_ref, k, pair[0], pair[1])
    for e in range(8):
        re, im = adjoint_child(xs_ref, wh_ref, wl_ref, e, level1_turn(both, e))
        for q, v in enumerate(quarters(re, im)):
            for p in range(2):
                start = (8 * p + e) * 16 + 4 * q
                out_ref[start : start + 4, :] = v[4 * p : 4 * p + 4]


def adjoint0(med_ref, x_ref, wh_ref, wl_ref, out_ref, xs_ref, mid_ref):
    med, grid = medium_of(med_ref), grid_points()
    r, rays = travel_rays(own_source(rows8()), 0.5, grid, med)
    table = patterns(0, rays)
    target = as_f32(digit_coords(rows8(), 1))
    for k in range(0, 8, 2):
        pair = [
            wide(x_ref, [(j >> 2) * 16 + c * 4 + (j & 3) for c in range(4)], 32)
            for j in (k, k + 1)
        ]
        adjoint_put(xs_ref, k, pair[0], pair[1])
    for e in range(8):
        re, im = adjoint_child(xs_ref, wh_ref, wl_ref, e, pick(table, e))
        one = slice(e, e + 1)
        c, s = root_turn(med, target, (r[one], [v[one] for v in rays]))
        for q, v in enumerate(quarters(re * c + im * s, im * c - re * s)):
            mid_ref[pl.ds(64 * q + e, 8, stride=8), :] = v
    pack(mid_ref, out_ref)


def call(kernel, name, out_shape, scratch, levels, *operands, space=pltpu.VMEM, room=16):
    return pl.pallas_call(
        kernel,
        out_shape=jax.ShapeDtypeStruct(out_shape, F32),
        in_specs=[pl.BlockSpec(memory_space=space)] * len(operands),
        out_specs=pl.BlockSpec(memory_space=pltpu.VMEM),
        scratch_shapes=scratch,
        compiler_params=pltpu.CompilerParams(vmem_limit_bytes=room * 2**20),
        cost_estimate=pl.CostEstimate(
            flops=levels * 10**9, bytes_accessed=2 * 10**6, transcendentals=0
        ),
        name=name,
    )(*operands)


CHUNK = 16


def shards(forward_weights, adjoint_weights, medium):
    wh, wl = (jnp.asarray(v) for v in tables())
    medium = medium.reshape(1, 4)
    fscr = pltpu.VMEM((256, 8 * W), BF16)
    ascr = pltpu.VMEM((256, W), BF16)
    mid = pltpu.VMEM((256, 128), F32)
    tail = pltpu.VMEM((64, 128), F32)
    swap = functools.partial(lax.all_to_all, split_axis=0, concat_axis=0, tiled=True)

    def over(x, axis, count):
        shape = x.shape
        return swap(x.reshape(count, shape[0] // count, 128), axis).reshape(shape)

    fw = forward_weights.reshape(64, 2 * Q)
    table = pltpu.VMEM((8 * W, W), BF16)
    own = [pltpu.VMEM((1, 4), F32), pltpu.VMEM((64, 2 * Q), F32), table, table]
    own.append(pltpu.SemaphoreType.DMA((2 + 2 * PIECES,)))
    f0 = call(
        forward0,
        "forward0",
        (256, 128),
        [fscr, tail] + own,
        1,
        medium,
        fw,
        wh,
        wl,
        space=pltpu.HBM,
        room=58,
    )
    f0 = over(f0, "sx", 16)
    a2 = call(
        adjoint32, "adjoint32", (256, 128), [ascr, mid, tail], 2, medium, adjoint_weights, wh, wl
    )
    f1 = functools.partial(forward1, CHUNK)
    both = call(f1, "forward1", (512, 128), [fscr], 1, medium, f0, wh, wl, a2)
    both = over(both, "sy", 32)
    a1 = functools.partial(adjoint1, CHUNK)
    a1 = call(a1, "adjoint1", (256, 128), [ascr], 1, medium, both, wh, wl)
    a1 = over(a1, "sx", 16)
    f3 = functools.partial(forward23, CHUNK)
    f3 = call(f3, "forward23", (64, 2 * Q), [fscr, mid], 2, medium, both, wh, wl)
    a0 = call(adjoint0, "adjoint0", (64, 2 * Q), [ascr, mid], 1, medium, a1, wh, wl)
    return f3, a0.reshape(8, 8, 2 * Q)


def solution(mesh):
    return jax.shard_map(
        shards,
        mesh=mesh,
        in_specs=(P(("sy", "sx"), None, None), P(("sx", "sy"), None), P()),
        out_specs=(P(("sx", "sy"), None), P(None, ("sy", "sx"), None)),
        check_vma=False,
    )
```

```python
import functools
import math

import jax
import jax.numpy as jnp
import numpy as np
from jax import lax
from jax.experimental import pallas as pl
from jax.experimental.pallas import tpu as pltpu
from jax.sharding import PartitionSpec as P

ORDER = 6
Q = 216
W = 256
F32 = jnp.float32
BF16 = jnp.bfloat16
PATTERNS = (7, 6, 5, 4)
KORD = (7, 0, 6, 1, 5, 2, 4, 3)
PIECES = 4
CUT = 2 * Q - 384
SPILL = Q - 128


def cheb_points():
    return np.array([(1.0 - math.cos((2 * i + 1) * math.pi / (2 * ORDER))) / 2.0 for i in range(ORDER)])


def child_table():
    nodes = cheb_points()
    halves = []
    for bit in range(2):
        matrix = np.zeros((ORDER, ORDER))
        for row in range(ORDER):
            where = (nodes[row] + bit) / 2.0
            for col in range(ORDER):
                value = 1.0
                for other in range(ORDER):
                    if other != col:
                        value *= (where - nodes[other]) / (nodes[col] - nodes[other])
                matrix[row, col] = value
        halves.append(matrix)
    return np.stack(
        [np.kron(np.kron(halves[e // 4], halves[e // 2 % 2]), halves[e % 2]) for e in range(8)]
    )


def tables():
    table = np.zeros((8, W, W))
    table[:, :Q, :Q] = child_table() / math.sqrt(8.0)
    whole = table.reshape(8 * W, W).astype(np.float32)
    high = whole.astype(jnp.bfloat16)
    return high, (whole - high.astype(np.float32)).astype(jnp.bfloat16)


def turn_polynomials():
    x = (np.cos(np.pi * (np.arange(400) + 0.5) / 400) + 1.0) / 8.0
    f = np.sqrt(x)
    s = np.polynomial.chebyshev.Chebyshev.fit(x, np.sin(2 * np.pi * f) / f, 5, domain=[0, 0.25])
    c = np.polynomial.chebyshev.Chebyshev.fit(x, np.cos(2 * np.pi * f), 6, domain=[0, 0.25])
    return [
        [float(v) for v in p.convert(kind=np.polynomial.Polynomial).coef] for p in (s, c)
    ]


SIN, COS = turn_polynomials()


def horner(coefs, z):
    value = jnp.full_like(z, coefs[-1])
    for c in coefs[-2::-1]:
        value = value * z + c
    return value


def cis(turns):
    f = turns - jnp.round(turns)
    z = f * f
    return horner(COS, z), f * horner(SIN, z)


def digit_coords(index, digits):
    out = []
    for bit in (2, 1, 0):
        value = None
        for d in range(digits):
            part = (index >> (3 * d + bit)) & 1
            part = part << d if d else part
            value = part if value is None else value + part
        out.append(value)
    return out


def as_f32(values):
    return [v.astype(F32) for v in values]


def rows8():
    return lax.broadcasted_iota(jnp.int32, (8, W), 0)


def grid_points():
    t = lax.broadcasted_iota(jnp.int32, (8, W), 1)
    i = (t * 7282) >> 18
    ij = (t * 10923) >> 16
    nodes = [float(v) for v in cheb_points()]
    out = []
    for n in (i, ij - 6 * i, t - 6 * ij):
        value = jnp.full((8, W), nodes[5], F32)
        for m in range(4, -1, -1):
            value = jnp.where(n == m, nodes[m], value)
        out.append(value)
    return out


def travel_rays(corner, side, grid, med):
    p = [side * (corner[d] + grid[d]) for d in range(3)]
    r = jnp.sqrt(p[0] * p[0] + p[1] * p[1] + p[2] * p[2])
    return r, [p[d] + med[d + 1] * r for d in range(3)]


def patterns(level, rays):
    step = 1.0 / 2 ** (level + 3)
    x, y, z = (step * v for v in rays)
    a, b = x + y, x - y
    return [cis(a + z), cis(a - z), cis(b + z), cis(b - z)]


def pick(table, row):
    return [(c[row : row + 1, :], s[row : row + 1, :]) for c, s in table]


def split16(first, second):
    whole = jnp.concatenate([first, second], axis=0)
    high = whole.astype(BF16)
    return high, (whole - high.astype(F32)).astype(BF16)


def forward_put(xs_ref, e, re, im, turn):
    cols = slice(e * W, (e + 1) * W)
    for s, (c, sn) in enumerate(turn):
        a, b, d, g = re * c, im * sn, im * c, re * sn
        for base, one, two in ((0, a - b, a + b), (64, d + g, d - g)):
            high, low = split16(one, two)
            row = base + 16 * s
            xs_ref[row : row + 16, cols] = high
            xs_ref[128 + row : 144 + row, cols] = low


def product(x, xh, wh, wl, side):
    dot = functools.partial(
        lax.dot_general, dimension_numbers=(((1,), (side,)), ((), ())), preferred_element_type=F32
    )
    both = dot(x, wh)
    return both[:128] + both[128:] + dot(xh, wl)


def forward_product(xs_ref, wh_ref, wl_ref):
    return product(xs_ref[...], xs_ref[0:128, :], wh_ref[...], wl_ref[...], 0)


def adjoint_put(xs_ref, k, first, second):
    for base, one, two in ((0, first[0], second[0]), (64, first[1], second[1])):
        high, low = split16(one, two)
        row = base + 8 * k
        xs_ref[row : row + 16, :] = high
        xs_ref[128 + row : 144 + row, :] = low


def adjoint_child(xs_ref, wh_ref, wl_ref, e, turn):
    cols = slice(e * W, (e + 1) * W)
    y = product(xs_ref[...], xs_ref[0:128, :], wh_ref[cols, :], wl_ref[cols, :], 1)
    re = im = None
    for k, (c, sn) in zip(PATTERNS, turn):
        o = 7 - k
        kr, ki = y[8 * k : 8 * k + 8], y[64 + 8 * k : 72 + 8 * k]
        br, bi = y[8 * o : 8 * o + 8], y[64 + 8 * o : 72 + 8 * o]
        one = c * (kr + br) + sn * (ki - bi)
        two = c * (ki + bi) - sn * (kr - br)
        re, im = (one, two) if re is None else (re + one, im + two)
    return re, im


def quarters(re, im):
    return re[:, :128], re[:, 128:], im[:, :128], im[:, 128:]


def join(a, b):
    return jnp.concatenate([a, b], axis=1)


def unpack(x_ref, tail_ref):
    tail_ref[...] = jnp.zeros_like(tail_ref)
    tail_ref[:, 0:CUT] = x_ref[:, 384 : 2 * Q]
    lane = lax.broadcasted_iota(jnp.int32, (64, 128), 1)
    x0, x1, x2, x3 = x_ref[:, 0:128], x_ref[:, 128:256], x_ref[:, 256:384], tail_ref[...]
    shift = 128 - SPILL
    r1, r2, r3 = (pltpu.roll(v, shift, 1) for v in (x1, x2, x3))
    re = join(x0, jnp.where(lane < SPILL, x1, 0.0))
    im = join(
        jnp.where(lane < shift, r1, r2),
        jnp.where(lane < shift, r2, jnp.where(lane < SPILL, r3, 0.0)),
    )
    return re, im


def pack(parts, out_ref):
    r0, r1, i0, i1 = (parts[64 * c : 64 * c + 64, :] for c in range(4))
    lane = lax.broadcasted_iota(jnp.int32, (64, 128), 1)
    s0, s1 = pltpu.roll(i0, SPILL, 1), pltpu.roll(i1, SPILL, 1)
    out_ref[:, 0:128] = r0
    out_ref[:, 128:256] = jnp.where(lane < SPILL, r1, s0)
    out_ref[:, 256:384] = jnp.where(lane < SPILL, s0, s1)
    out_ref[:, 384 : 2 * Q] = s1[:, 0:CUT]


def lanes(shape):
    return lax.broadcasted_iota(jnp.int32, shape, 1)


def spread(t3, rows):
    own = lanes(rows[0].shape) < SPILL
    return [
        jnp.where(own, row, pltpu.roll(t, shift, 1))
        for row, t, shift in zip(rows, t3, (SPILL, SPILL - 40, SPILL - 80))
    ]


def gather3(rows):
    a, b, c = (pltpu.roll(v, s, 1) for v, s in zip(rows, (40, 80, 120)))
    lane = lanes(a.shape)
    return jnp.where(lane < 40, a, jnp.where(lane < 80, b, c))


def medium_of(med_ref):
    return [jnp.broadcast_to(med_ref[0:1, i : i + 1], (8, W)) for i in range(4)]


def own_source(extra_rows):
    own = lax.axis_index("sy") * 16 + lax.axis_index("sx")
    high = digit_coords(own, 3)
    low = digit_coords(extra_rows, 1)
    return as_f32([low[d] + 2 * high[d] for d in range(3)])


def root_turn(med, corner, rays0):
    r, rays = rays0
    centre = [(v + 0.5) * 0.5 for v in corner]
    travel = med[0] * r
    return cis(travel + centre[0] * rays[0] + centre[1] * rays[1] + centre[2] * rays[2])


def end_turn(med, block, across, grid):
    own = lax.axis_index("sx") * 32 + lax.axis_index("sy")
    high = digit_coords(own, 3)
    row = digit_coords(rows8(), 1)
    fixed = digit_coords(block, 1)
    wr, wf = (1, 2) if across else (2, 1)
    centre = [
        ((4 * high[d] + wf * fixed[d] + wr * row[d]).astype(F32) + 0.5) * (1.0 / 32.0)
        for d in range(3)
    ]
    p = [8.0 * grid[d] for d in range(3)]
    r = jnp.sqrt(p[0] * p[0] + p[1] * p[1] + p[2] * p[2])
    u = med[0] * r
    for d in range(3):
        u = u + centre[d] * (p[d] + med[d + 1] * r)
    return cis(u)


def level_patterns(level, corner, side, grid, med):
    return patterns(level, travel_rays(corner, side, grid, med)[1])


def level1_tables(grid, med):
    high = digit_coords(lax.axis_index("sy") * 2, 2)
    first = digit_coords(rows8(), 1)
    out = []
    for half in range(2):
        mid = digit_coords(lax.axis_index("sy") * 2 + half, 2)
        corner = as_f32([first[d] + 2 * mid[d] for d in range(3)])
        out.append(level_patterns(1, corner, 1.0, grid, med))
    return out


def level1_turn(both, e):
    upper = rows8() < 4
    return [
        (
            jnp.where(upper, c0[e : e + 1, :], c1[e : e + 1, :]),
            jnp.where(upper, s0[e : e + 1, :], s1[e : e + 1, :]),
        )
        for (c0, s0), (c1, s1) in zip(*both)
    ]


def level2_turn(e, grid, med):
    parent = digit_coords(rows8(), 1)
    child = digit_coords(e, 1)
    corner = as_f32([2 * parent[d] + child[d] for d in range(3)])
    return level_patterns(2, corner, 2.0, grid, med)


def level3_table(grid, med):
    return level_patterns(3, as_f32(digit_coords(rows8(), 1)), 4.0, grid, med)


def rows_of(ref, start, stride, count=8):
    return ref[pl.ds(start, count, stride=stride), :]


def wide(ref, start, stride):
    return join(rows_of(ref, start[0], stride), rows_of(ref, start[1], stride)), join(
        rows_of(ref, start[2], stride), rows_of(ref, start[3], stride)
    )


def forward0(med_hbm, x_hbm, wh_hbm, wl_hbm, out_ref, xs_ref, tail_ref, med_ref, x_ref, wh_ref, wl_ref, sems):
    copies = [
        pltpu.make_async_copy(med_hbm, med_ref, sems.at[0]),
        pltpu.make_async_copy(x_hbm, x_ref, sems.at[1]),
    ]
    step = 8 * W // PIECES
    for i, (src, dst) in enumerate(((wh_hbm, wh_ref), (wl_hbm, wl_ref))):
        for j in range(PIECES):
            part = pl.ds(step * j, step)
            copies.append(
                pltpu.make_async_copy(src.at[part, :], dst.at[part, :], sems.at[2 + PIECES * i + j])
            )
    for copy in copies:
        copy.start()
    copies[0].wait()
    med, grid = medium_of(med_ref), grid_points()
    r, rays = travel_rays(own_source(rows8()), 0.5, grid, med)
    table = patterns(0, rays)
    target = as_f32(digit_coords(rows8(), 1))
    turns = []
    for e in range(8):
        one = slice(e, e + 1)
        turns.append(root_turn(med, target, (r[one], [v[one] for v in rays])))
    copies[1].wait()
    re, im = unpack(x_ref, tail_ref)
    for e in range(8):
        c, s = turns[e]
        xr, xi = re[8 * e : 8 * e + 8], im[8 * e : 8 * e + 8]
        forward_put(xs_ref, e, xr * c - xi * s, xr * s + xi * c, pick(table, e))
    for copy in copies[2:]:
        copy.wait()
    y = forward_product(xs_ref, wh_ref, wl_ref)
    for pos, k in enumerate(KORD):
        four = quarters(y[8 * pos : 8 * pos + 8], y[64 + 8 * pos : 72 + 8 * pos])
        for c, v in enumerate(four):
            out_ref[pl.ds((k >> 2) * 16 + c * 4 + (k & 3), 8, stride=32), :] = v


def forward1(med_ref, x_ref, wh_ref, wl_ref, other_ref, out_ref, xs_ref):
    for q in range(7):
        for group in range(0, 32, 8):
            out_ref[pl.ds(group * 14 + 7 + q, 8, stride=14), :] = other_ref[
                q * 32 + group : q * 32 + group + 8, :
            ]
    med, grid = medium_of(med_ref), grid_points()
    both = level1_tables(grid, med)
    upper = lax.broadcasted_iota(jnp.int32, (8, 128), 0) < 4
    for e in range(8):
        halves = []
        for part in range(2):
            t0 = x_ref[e * 16 + 8 * part : e * 16 + 8 * part + 8, :]
            t1 = x_ref[128 + e * 16 + 8 * part : 128 + e * 16 + 8 * part + 8, :]
            halves.append(
                join(
                    jnp.where(upper, t0, pltpu.roll(t1, 4, 0)),
                    jnp.where(upper, pltpu.roll(t0, 4, 0), t1),
                )
            )
        forward_put(xs_ref, e, halves[0], halves[1], level1_turn(both, e))
    y = forward_product(xs_ref, wh_ref, wl_ref)
    for pos, k in enumerate(KORD):
        r0, r1, i0, i1 = quarters(y[8 * pos : 8 * pos + 8], y[64 + 8 * pos : 72 + 8 * pos])
        last = pltpu.roll(i1, 4, 0)
        u4, u5, u6 = spread((last, last, i1), (r1, i1, r1))
        low, high = slice(0, 4), slice(4, 8)
        rows = (r0[low], i0[low], r0[high], i0[high], u4[low], u5[low], u6[high])
        for q, v in enumerate(rows):
            out_ref[pl.ds(k * 14 + q, 4, stride=112), :] = v


def forward23(med_ref, x_ref, wh_ref, wl_ref, out_ref, xs_ref, mid_ref):
    med, grid = medium_of(med_ref), grid_points()
    for m in range(4):
        row = [rows_of(x_ref, m * 14 + q, 56) for q in range(7)]
        pair = (
            (join(row[0], row[4]), join(row[1], row[5])),
            (join(row[2], row[6]), join(row[3], gather3(row[4:]))),
        )
        for e, (re, im) in zip((2 * m, 2 * m + 1), pair):
            forward_put(xs_ref, e, re, im, level2_turn(e, grid, med))
    y = forward_product(xs_ref, wh_ref, wl_ref)
    for pos, k in enumerate(KORD):
        four = quarters(y[8 * pos : 8 * pos + 8], y[64 + 8 * pos : 72 + 8 * pos])
        for c, v in enumerate(four):
            mid_ref[64 * c + 8 * k : 64 * c + 8 * k + 8, :] = v
    table = level3_table(grid, med)
    for e in range(8):
        re, im = wide(mid_ref, [64 * c + e for c in range(4)], 8)
        forward_put(xs_ref, e, re, im, pick(table, e))
    y = forward_product(xs_ref, wh_ref, wl_ref)
    for pos, k in enumerate(KORD):
        c, s = end_turn(med, k, False, grid)
        re, im = y[8 * pos : 8 * pos + 8], y[64 + 8 * pos : 72 + 8 * pos]
        four = quarters(re * c + im * s, im * c - re * s)
        for q, v in enumerate(four):
            mid_ref[pl.ds(64 * q + k, 8, stride=8), :] = v
    pack(mid_ref, out_ref)


def adjoint32(med_ref, x_ref, wh_ref, wl_ref, out_ref, xs_ref, mid_ref, tail_ref):
    med, grid = medium_of(med_ref), grid_points()
    re, im = unpack(x_ref, tail_ref)
    for k in range(8):
        c, s = end_turn(med, k, True, grid)
        xr, xi = re[8 * k : 8 * k + 8], im[8 * k : 8 * k + 8]
        for q, v in enumerate(quarters(xr * c - xi * s, xr * s + xi * c)):
            mid_ref[64 * q + 8 * k : 64 * q + 8 * k + 8, :] = v
    for k in range(0, 8, 2):
        adjoint_put(
            xs_ref,
            k,
            wide(mid_ref, [64 * c + k for c in range(4)], 8),
            wide(mid_ref, [64 * c + k + 1 for c in range(4)], 8),
        )
    table = level3_table(grid, med)
    for e in range(8):
        re, im = adjoint_child(xs_ref, wh_ref, wl_ref, e, pick(table, e))
        for q, v in enumerate(quarters(re, im)):
            mid_ref[pl.ds(64 * q + e, 8, stride=8), :] = v
    for k in range(0, 8, 2):
        pair = []
        for j in (k, k + 1):
            r0, r1, i0, i1 = (mid_ref[64 * c + 8 * j : 64 * c + 8 * j + 8, :] for c in range(4))
            pair.append((join(r0, r1), join(i0, i1)))
        adjoint_put(xs_ref, k, pair[0], pair[1])
    for m in range(4):
        first, second = (
            quarters(*adjoint_child(xs_ref, wh_ref, wl_ref, e, level2_turn(e, grid, med)))
            for e in (2 * m, 2 * m + 1)
        )
        tails = spread((second[3],) * 3, (first[1], first[3], second[1]))
        for q, v in enumerate((first[0], first[2], second[0], second[2], *tails)):
            out_ref[pl.ds(q * 32 + m, 8, stride=4), :] = v


def adjoint1(med_ref, x_ref, wh_ref, wl_ref, out_ref, xs_ref):
    med, grid = medium_of(med_ref), grid_points()
    both = level1_tables(grid, med)
    for k in range(0, 8, 2):
        pair = []
        for j in (k, k + 1):
            row = [rows_of(x_ref, j * 14 + 7 + q, 112, 4) for q in range(7)]
            t3 = gather3(row[4:])
            four = [
                jnp.concatenate(v, axis=0)
                for v in ((row[0], row[2]), (row[4], row[6]), (row[1], row[3]), (row[5], t3))
            ]
            pair.append((join(four[0], four[1]), join(four[2], four[3])))
        adjoint_put(xs_ref, k, pair[0], pair[1])
    for e in range(8):
        re, im = adjoint_child(xs_ref, wh_ref, wl_ref, e, level1_turn(both, e))
        for q, v in enumerate(quarters(re, im)):
            for p in range(2):
                start = (8 * p + e) * 16 + 4 * q
                out_ref[start : start + 4, :] = v[4 * p : 4 * p + 4]


def adjoint0(med_ref, x_ref, wh_ref, wl_ref, out_ref, xs_ref, mid_ref):
    med, grid = medium_of(med_ref), grid_points()
    r, rays = travel_rays(own_source(rows8()), 0.5, grid, med)
    table = patterns(0, rays)
    target = as_f32(digit_coords(rows8(), 1))
    for k in range(0, 8, 2):
        pair = [
            wide(x_ref, [(j >> 2) * 16 + c * 4 + (j & 3) for c in range(4)], 32)
            for j in (k, k + 1)
        ]
        adjoint_put(xs_ref, k, pair[0], pair[1])
    for e in range(8):
        re, im = adjoint_child(xs_ref, wh_ref, wl_ref, e, pick(table, e))
        one = slice(e, e + 1)
        c, s = root_turn(med, target, (r[one], [v[one] for v in rays]))
        for q, v in enumerate(quarters(re * c + im * s, im * c - re * s)):
            mid_ref[pl.ds(64 * q + e, 8, stride=8), :] = v
    pack(mid_ref, out_ref)


def call(kernel, name, out_shape, scratch, levels, *operands, space=pltpu.VMEM, room=16):
    return pl.pallas_call(
        kernel,
        out_shape=jax.ShapeDtypeStruct(out_shape, F32),
        in_specs=[pl.BlockSpec(memory_space=space)] * len(operands),
        out_specs=pl.BlockSpec(memory_space=pltpu.VMEM),
        scratch_shapes=scratch,
        compiler_params=pltpu.CompilerParams(vmem_limit_bytes=room * 2**20),
        cost_estimate=pl.CostEstimate(
            flops=levels * 10**9, bytes_accessed=2 * 10**6, transcendentals=0
        ),
        name=name,
    )(*operands)


def shards(forward_weights, adjoint_weights, medium):
    wh, wl = (jnp.asarray(v) for v in tables())
    medium = medium.reshape(1, 4)
    fscr = pltpu.VMEM((256, 8 * W), BF16)
    ascr = pltpu.VMEM((256, W), BF16)
    mid = pltpu.VMEM((256, 128), F32)
    tail = pltpu.VMEM((64, 128), F32)
    swap = functools.partial(lax.all_to_all, split_axis=0, concat_axis=0, tiled=True)

    def over(x, axis, count, rows):
        shape = x.shape
        return swap(x.reshape(count, -1, rows, 128), axis).reshape(shape)

    fw = forward_weights.reshape(64, 2 * Q)
    table = pltpu.VMEM((8 * W, W), BF16)
    own = [pltpu.VMEM((1, 4), F32), pltpu.VMEM((64, 2 * Q), F32), table, table]
    own.append(pltpu.SemaphoreType.DMA((2 + 2 * PIECES,)))
    f0 = call(
        forward0,
        "forward0",
        (256, 128),
        [fscr, tail] + own,
        1,
        medium,
        fw,
        wh,
        wl,
        space=pltpu.HBM,
        room=58,
    )
    f0 = over(f0, "sx", 16, 8)
    a2 = call(
        adjoint32, "adjoint32", (224, 128), [ascr, mid, tail], 2, medium, adjoint_weights, wh, wl
    )
    both = call(forward1, "forward1", (448, 128), [fscr], 1, medium, f0, wh, wl, a2)
    both = over(both, "sy", 32, 2)
    a1 = call(adjoint1, "adjoint1", (256, 128), [ascr], 1, medium, both, wh, wl)
    a1 = over(a1, "sx", 16, 8)
    f3 = call(forward23, "forward23", (64, 2 * Q), [fscr, mid], 2, medium, both, wh, wl)
    a0 = call(adjoint0, "adjoint0", (64, 2 * Q), [ascr, mid], 1, medium, a1, wh, wl)
    return f3, a0.reshape(8, 8, 2 * Q)


def solution(mesh):
    return jax.shard_map(
        shards,
        mesh=mesh,
        in_specs=(P(("sy", "sx"), None, None), P(("sx", "sy"), None), P()),
        out_specs=(P(("sx", "sy"), None), P(None, ("sy", "sx"), None)),
        check_vma=False,
    )
```

```python
import functools
import math

import jax
import jax.numpy as jnp
import numpy as np
from jax import lax
from jax.experimental import pallas as pl
from jax.experimental.pallas import tpu as pltpu
from jax.sharding import PartitionSpec as P

ORDER = 6
Q = 216
W = 256
F32 = jnp.float32
BF16 = jnp.bfloat16
PATTERNS = (7, 6, 5, 4)
KORD = (7, 0, 6, 1, 5, 2, 4, 3)
CUT = 2 * Q - 384
SPILL = Q - 128


def cheb_points():
    return np.array([(1.0 - math.cos((2 * i + 1) * math.pi / (2 * ORDER))) / 2.0 for i in range(ORDER)])


def child_halves():
    nodes = cheb_points()
    halves = []
    for bit in range(2):
        matrix = np.zeros((ORDER, ORDER))
        for row in range(ORDER):
            where = (nodes[row] + bit) / 2.0
            for col in range(ORDER):
                value = 1.0
                for other in range(ORDER):
                    if other != col:
                        value *= (where - nodes[other]) / (nodes[col] - nodes[other])
                matrix[row, col] = value
        halves.append(matrix)
    return halves


def child_table():
    halves = child_halves()
    return np.stack(
        [np.kron(np.kron(halves[e // 4], halves[e // 2 % 2]), halves[e % 2]) for e in range(8)]
    )


def tables():
    table = np.zeros((8, W, W))
    table[:, :Q, :Q] = child_table() / math.sqrt(8.0)
    whole = table.reshape(8 * W, W).astype(np.float32)
    high = whole.astype(jnp.bfloat16)
    return high, (whole - high.astype(np.float32)).astype(jnp.bfloat16)


def turn_polynomials():
    x = (np.cos(np.pi * (np.arange(400) + 0.5) / 400) + 1.0) / 8.0
    f = np.sqrt(x)
    s = np.polynomial.chebyshev.Chebyshev.fit(x, np.sin(2 * np.pi * f) / f, 5, domain=[0, 0.25])
    c = np.polynomial.chebyshev.Chebyshev.fit(x, np.cos(2 * np.pi * f), 6, domain=[0, 0.25])
    return [
        [float(v) for v in p.convert(kind=np.polynomial.Polynomial).coef] for p in (s, c)
    ]


SIN, COS = turn_polynomials()


def horner(coefs, z):
    value = jnp.full_like(z, coefs[-1])
    for c in coefs[-2::-1]:
        value = value * z + c
    return value


def cis(turns):
    f = turns - jnp.round(turns)
    z = f * f
    return horner(COS, z), f * horner(SIN, z)


def digit_coords(index, digits):
    out = []
    for bit in (2, 1, 0):
        value = None
        for d in range(digits):
            part = (index >> (3 * d + bit)) & 1
            part = part << d if d else part
            value = part if value is None else value + part
        out.append(value)
    return out


def as_f32(values):
    return [v.astype(F32) for v in values]


def rows8():
    return lax.broadcasted_iota(jnp.int32, (8, W), 0)


def point_digits(t):
    i = (t * 7282) >> 18
    ij = (t * 10923) >> 16
    return i, ij - 6 * i, t - 6 * ij


def build_tables(wh_ref, wl_ref):
    lane = lax.broadcasted_iota(jnp.int32, (W, 128), 1)
    wanted = jnp.where(lane < 24, lane & 7, 8)
    picks = [
        jnp.where(n == wanted, 1.0, 0.0).astype(BF16)
        for n in point_digits(lax.broadcasted_iota(jnp.int32, (W, 128), 0))
    ]
    digits = point_digits(lax.broadcasted_iota(jnp.int32, (8, W), 1))
    row = rows8()
    factors = [[], [], []]
    for half in child_halves():
        rest = half / math.sqrt(2.0)
        pieces = [[], [], []]
        for _ in range(3):
            piece = rest.astype(jnp.bfloat16).astype(np.float64)
            rest = rest - piece
            columns = []
            for i in range(ORDER):
                column = jnp.zeros((8, W), F32)
                for m in range(ORDER):
                    column = jnp.where(row == m, float(piece[m, i]), column)
                columns.append(column)
            for d in range(3):
                value = jnp.zeros((8, W), F32)
                for i in range(ORDER):
                    value = jnp.where(digits[d] == i, columns[i], value)
                pieces[d].append(value)
        for d in range(3):
            spread_rows = jnp.concatenate(pieces[d] + [jnp.zeros((104, W), F32)], axis=0)
            factors[d].append(
                jnp.dot(picks[d], spread_rows.astype(BF16), preferred_element_type=F32)
            )
    for yz in range(4):
        part = factors[1][yz >> 1] * factors[2][yz & 1]
        for x in range(2):
            whole = factors[0][x] * part
            high = whole.astype(BF16)
            rows = slice((4 * x + yz) * W, (4 * x + yz + 1) * W)
            wh_ref[rows, :] = high
            wl_ref[rows, :] = (whole - high.astype(F32)).astype(BF16)


def grid_points():
    t = lax.broadcasted_iota(jnp.int32, (8, W), 1)
    nodes = [float(v) for v in cheb_points()]
    out = []
    for n in point_digits(t):
        value = jnp.full((8, W), nodes[5], F32)
        for m in range(4, -1, -1):
            value = jnp.where(n == m, nodes[m], value)
        out.append(value)
    return out


def travel_rays(corner, side, grid, med):
    p = [side * (corner[d] + grid[d]) for d in range(3)]
    r = jnp.sqrt(p[0] * p[0] + p[1] * p[1] + p[2] * p[2])
    return r, [p[d] + med[d + 1] * r for d in range(3)]


def patterns(level, rays):
    step = 1.0 / 2 ** (level + 3)
    x, y, z = (step * v for v in rays)
    a, b = x + y, x - y
    return [cis(a + z), cis(a - z), cis(b + z), cis(b - z)]


def pick(table, row):
    return [(c[row : row + 1, :], s[row : row + 1, :]) for c, s in table]


def split16(first, second):
    whole = jnp.concatenate([first, second], axis=0)
    high = whole.astype(BF16)
    return high, (whole - high.astype(F32)).astype(BF16)


def forward_put(xs_ref, e, re, im, turn):
    cols = slice(e * W, (e + 1) * W)
    for s, (c, sn) in enumerate(turn):
        a, b, d, g = re * c, im * sn, im * c, re * sn
        for base, one, two in ((0, a - b, a + b), (64, d + g, d - g)):
            high, low = split16(one, two)
            row = base + 16 * s
            xs_ref[row : row + 16, cols] = high
            xs_ref[128 + row : 144 + row, cols] = low


def product(x, xh, wh, wl, side):
    dot = functools.partial(
        lax.dot_general, dimension_numbers=(((1,), (side,)), ((), ())), preferred_element_type=F32
    )
    both = dot(x, wh)
    return both[:128] + both[128:] + dot(xh, wl)


def forward_product(xs_ref, wh_ref, wl_ref):
    return product(xs_ref[...], xs_ref[0:128, :], wh_ref[...], wl_ref[...], 0)


def adjoint_put(xs_ref, k, first, second):
    for base, one, two in ((0, first[0], second[0]), (64, first[1], second[1])):
        high, low = split16(one, two)
        row = base + 8 * k
        xs_ref[row : row + 16, :] = high
        xs_ref[128 + row : 144 + row, :] = low


def adjoint_child(xs_ref, wh_ref, wl_ref, e, turn):
    cols = slice(e * W, (e + 1) * W)
    y = product(xs_ref[...], xs_ref[0:128, :], wh_ref[cols, :], wl_ref[cols, :], 1)
    re = im = None
    for k, (c, sn) in zip(PATTERNS, turn):
        o = 7 - k
        kr, ki = y[8 * k : 8 * k + 8], y[64 + 8 * k : 72 + 8 * k]
        br, bi = y[8 * o : 8 * o + 8], y[64 + 8 * o : 72 + 8 * o]
        one = c * (kr + br) + sn * (ki - bi)
        two = c * (ki + bi) - sn * (kr - br)
        re, im = (one, two) if re is None else (re + one, im + two)
    return re, im


def quarters(re, im):
    return re[:, :128], re[:, 128:], im[:, :128], im[:, 128:]


def join(a, b):
    return jnp.concatenate([a, b], axis=1)


def unpack(x_ref, tail_ref):
    tail_ref[...] = jnp.zeros_like(tail_ref)
    tail_ref[:, 0:CUT] = x_ref[:, 384 : 2 * Q]
    lane = lax.broadcasted_iota(jnp.int32, (64, 128), 1)
    x0, x1, x2, x3 = x_ref[:, 0:128], x_ref[:, 128:256], x_ref[:, 256:384], tail_ref[...]
    shift = 128 - SPILL
    r1, r2, r3 = (pltpu.roll(v, shift, 1) for v in (x1, x2, x3))
    re = join(x0, jnp.where(lane < SPILL, x1, 0.0))
    im = join(
        jnp.where(lane < shift, r1, r2),
        jnp.where(lane < shift, r2, jnp.where(lane < SPILL, r3, 0.0)),
    )
    return re, im


def pack(parts, out_ref):
    r0, r1, i0, i1 = (parts[64 * c : 64 * c + 64, :] for c in range(4))
    lane = lax.broadcasted_iota(jnp.int32, (64, 128), 1)
    s0, s1 = pltpu.roll(i0, SPILL, 1), pltpu.roll(i1, SPILL, 1)
    out_ref[:, 0:128] = r0
    out_ref[:, 128:256] = jnp.where(lane < SPILL, r1, s0)
    out_ref[:, 256:384] = jnp.where(lane < SPILL, s0, s1)
    out_ref[:, 384 : 2 * Q] = s1[:, 0:CUT]


def lanes(shape):
    return lax.broadcasted_iota(jnp.int32, shape, 1)


def spread(t3, rows):
    own = lanes(rows[0].shape) < SPILL
    return [
        jnp.where(own, row, pltpu.roll(t, shift, 1))
        for row, t, shift in zip(rows, t3, (SPILL, SPILL - 40, SPILL - 80))
    ]


def gather3(rows):
    a, b, c = (pltpu.roll(v, s, 1) for v, s in zip(rows, (40, 80, 120)))
    lane = lanes(a.shape)
    return jnp.where(lane < 40, a, jnp.where(lane < 80, b, c))


def medium_of(med_ref):
    return [jnp.broadcast_to(med_ref[0:1, i : i + 1], (8, W)) for i in range(4)]


def own_source(extra_rows):
    own = lax.axis_index("sy") * 16 + lax.axis_index("sx")
    high = digit_coords(own, 3)
    low = digit_coords(extra_rows, 1)
    return as_f32([low[d] + 2 * high[d] for d in range(3)])


def root_turn(med, corner, rays0):
    r, rays = rays0
    centre = [(v + 0.5) * 0.5 for v in corner]
    travel = med[0] * r
    return cis(travel + centre[0] * rays[0] + centre[1] * rays[1] + centre[2] * rays[2])


def end_turn(med, block, across, grid):
    own = lax.axis_index("sx") * 32 + lax.axis_index("sy")
    high = digit_coords(own, 3)
    row = digit_coords(rows8(), 1)
    fixed = digit_coords(block, 1)
    wr, wf = (1, 2) if across else (2, 1)
    centre = [
        ((4 * high[d] + wf * fixed[d] + wr * row[d]).astype(F32) + 0.5) * (1.0 / 32.0)
        for d in range(3)
    ]
    p = [8.0 * grid[d] for d in range(3)]
    r = jnp.sqrt(p[0] * p[0] + p[1] * p[1] + p[2] * p[2])
    u = med[0] * r
    for d in range(3):
        u = u + centre[d] * (p[d] + med[d + 1] * r)
    return cis(u)


def level_patterns(level, corner, side, grid, med):
    return patterns(level, travel_rays(corner, side, grid, med)[1])


def level1_tables(grid, med):
    high = digit_coords(lax.axis_index("sy") * 2, 2)
    first = digit_coords(rows8(), 1)
    out = []
    for half in range(2):
        mid = digit_coords(lax.axis_index("sy") * 2 + half, 2)
        corner = as_f32([first[d] + 2 * mid[d] for d in range(3)])
        out.append(level_patterns(1, corner, 1.0, grid, med))
    return out


def level1_turn(both, e):
    upper = rows8() < 4
    return [
        (
            jnp.where(upper, c0[e : e + 1, :], c1[e : e + 1, :]),
            jnp.where(upper, s0[e : e + 1, :], s1[e : e + 1, :]),
        )
        for (c0, s0), (c1, s1) in zip(*both)
    ]


def level2_turn(e, grid, med):
    parent = digit_coords(rows8(), 1)
    child = digit_coords(e, 1)
    corner = as_f32([2 * parent[d] + child[d] for d in range(3)])
    return level_patterns(2, corner, 2.0, grid, med)


def level3_table(grid, med):
    return level_patterns(3, as_f32(digit_coords(rows8(), 1)), 4.0, grid, med)


def keep(ref, slot, turn):
    for i, value in enumerate(v for pair in turn for v in pair):
        ref[8 * (slot + i) : 8 * (slot + i) + 8, :] = value


def kept(ref, slot, count):
    rows = [ref[8 * (slot + i) : 8 * (slot + i) + 8, :] for i in range(2 * count)]
    return list(zip(rows[::2], rows[1::2]))


def rows_of(ref, start, stride, count=8):
    return ref[pl.ds(start, count, stride=stride), :]


def wide(ref, start, stride):
    return join(rows_of(ref, start[0], stride), rows_of(ref, start[1], stride)), join(
        rows_of(ref, start[2], stride), rows_of(ref, start[3], stride)
    )


def forward0(med_hbm, x_hbm, out_ref, xs_ref, tail_ref, med_ref, x_ref, wh_ref, wl_ref, sems):
    copies = [
        pltpu.make_async_copy(med_hbm, med_ref, sems.at[0]),
        pltpu.make_async_copy(x_hbm, x_ref, sems.at[1]),
    ]
    for copy in copies:
        copy.start()
    build_tables(wh_ref, wl_ref)
    copies[0].wait()
    med, grid = medium_of(med_ref), grid_points()
    r, rays = travel_rays(own_source(rows8()), 0.5, grid, med)
    table = patterns(0, rays)
    target = as_f32(digit_coords(rows8(), 1))
    turns = []
    for e in range(8):
        one = slice(e, e + 1)
        turns.append(root_turn(med, target, (r[one], [v[one] for v in rays])))
    copies[1].wait()
    re, im = unpack(x_ref, tail_ref)
    for e in range(8):
        c, s = turns[e]
        xr, xi = re[8 * e : 8 * e + 8], im[8 * e : 8 * e + 8]
        forward_put(xs_ref, e, xr * c - xi * s, xr * s + xi * c, pick(table, e))
    y = forward_product(xs_ref, wh_ref, wl_ref)
    for pos, k in enumerate(KORD):
        four = quarters(y[8 * pos : 8 * pos + 8], y[64 + 8 * pos : 72 + 8 * pos])
        for c, v in enumerate(four):
            out_ref[pl.ds((k >> 2) * 16 + c * 4 + (k & 3), 8, stride=32), :] = v


def forward1(x_ref, wh_ref, wl_ref, other_ref, turn_ref, out_ref, xs_ref):
    for q in range(7):
        for group in range(0, 32, 8):
            out_ref[pl.ds(group * 14 + 7 + q, 8, stride=14), :] = other_ref[
                q * 32 + group : q * 32 + group + 8, :
            ]
    upper = lax.broadcasted_iota(jnp.int32, (8, 128), 0) < 4
    for e in range(8):
        halves = []
        for part in range(2):
            t0 = x_ref[e * 16 + 8 * part : e * 16 + 8 * part + 8, :]
            t1 = x_ref[128 + e * 16 + 8 * part : 128 + e * 16 + 8 * part + 8, :]
            halves.append(
                join(
                    jnp.where(upper, t0, pltpu.roll(t1, 4, 0)),
                    jnp.where(upper, pltpu.roll(t0, 4, 0), t1),
                )
            )
        forward_put(xs_ref, e, halves[0], halves[1], kept(turn_ref, 8 * e, 4))
    y = forward_product(xs_ref, wh_ref, wl_ref)
    for pos, k in enumerate(KORD):
        r0, r1, i0, i1 = quarters(y[8 * pos : 8 * pos + 8], y[64 + 8 * pos : 72 + 8 * pos])
        last = pltpu.roll(i1, 4, 0)
        u4, u5, u6 = spread((last, last, i1), (r1, i1, r1))
        low, high = slice(0, 4), slice(4, 8)
        rows = (r0[low], i0[low], r0[high], i0[high], u4[low], u5[low], u6[high])
        for q, v in enumerate(rows):
            out_ref[pl.ds(k * 14 + q, 4, stride=112), :] = v


def forward23(med_ref, x_ref, wh_ref, wl_ref, out_ref, turn_ref, xs_ref, mid_ref):
    med, grid = medium_of(med_ref), grid_points()
    for m in range(4):
        row = [rows_of(x_ref, m * 14 + q, 56) for q in range(7)]
        pair = (
            (join(row[0], row[4]), join(row[1], row[5])),
            (join(row[2], row[6]), join(row[3], gather3(row[4:]))),
        )
        for e, (re, im) in zip((2 * m, 2 * m + 1), pair):
            forward_put(xs_ref, e, re, im, level2_turn(e, grid, med))
    y = forward_product(xs_ref, wh_ref, wl_ref)
    for pos, k in enumerate(KORD):
        four = quarters(y[8 * pos : 8 * pos + 8], y[64 + 8 * pos : 72 + 8 * pos])
        for c, v in enumerate(four):
            mid_ref[64 * c + 8 * k : 64 * c + 8 * k + 8, :] = v
    table = level3_table(grid, med)
    for e in range(8):
        re, im = wide(mid_ref, [64 * c + e for c in range(4)], 8)
        forward_put(xs_ref, e, re, im, pick(table, e))
    y = forward_product(xs_ref, wh_ref, wl_ref)
    for pos, k in enumerate(KORD):
        c, s = end_turn(med, k, False, grid)
        re, im = y[8 * pos : 8 * pos + 8], y[64 + 8 * pos : 72 + 8 * pos]
        four = quarters(re * c + im * s, im * c - re * s)
        for q, v in enumerate(four):
            mid_ref[pl.ds(64 * q + k, 8, stride=8), :] = v
    pack(mid_ref, out_ref)
    r, rays = travel_rays(own_source(rows8()), 0.5, grid, med)
    keep(turn_ref, 0, patterns(0, rays))
    target = as_f32(digit_coords(rows8(), 1))
    for e in range(8):
        one = slice(e, e + 1)
        keep(turn_ref, 8 + 2 * e, [root_turn(med, target, (r[one], [v[one] for v in rays]))])


def adjoint32(med_ref, x_ref, wh_ref, wl_ref, out_ref, turn_ref, xs_ref, mid_ref, tail_ref):
    med, grid = medium_of(med_ref), grid_points()
    re, im = unpack(x_ref, tail_ref)
    for k in range(8):
        c, s = end_turn(med, k, True, grid)
        xr, xi = re[8 * k : 8 * k + 8], im[8 * k : 8 * k + 8]
        for q, v in enumerate(quarters(xr * c - xi * s, xr * s + xi * c)):
            mid_ref[64 * q + 8 * k : 64 * q + 8 * k + 8, :] = v
    for k in range(0, 8, 2):
        adjoint_put(
            xs_ref,
            k,
            wide(mid_ref, [64 * c + k for c in range(4)], 8),
            wide(mid_ref, [64 * c + k + 1 for c in range(4)], 8),
        )
    table = level3_table(grid, med)
    for e in range(8):
        re, im = adjoint_child(xs_ref, wh_ref, wl_ref, e, pick(table, e))
        for q, v in enumerate(quarters(re, im)):
            mid_ref[pl.ds(64 * q + e, 8, stride=8), :] = v
    for k in range(0, 8, 2):
        pair = []
        for j in (k, k + 1):
            r0, r1, i0, i1 = (mid_ref[64 * c + 8 * j : 64 * c + 8 * j + 8, :] for c in range(4))
            pair.append((join(r0, r1), join(i0, i1)))
        adjoint_put(xs_ref, k, pair[0], pair[1])
    for m in range(4):
        first, second = (
            quarters(*adjoint_child(xs_ref, wh_ref, wl_ref, e, level2_turn(e, grid, med)))
            for e in (2 * m, 2 * m + 1)
        )
        tails = spread((second[3],) * 3, (first[1], first[3], second[1]))
        for q, v in enumerate((first[0], first[2], second[0], second[2], *tails)):
            out_ref[pl.ds(q * 32 + m, 8, stride=4), :] = v
    both = level1_tables(grid, med)
    for e in range(8):
        keep(turn_ref, 8 * e, level1_turn(both, e))


def adjoint1(x_ref, wh_ref, wl_ref, turn_ref, out_ref, xs_ref):
    for k in range(0, 8, 2):
        pair = []
        for j in (k, k + 1):
            row = [rows_of(x_ref, j * 14 + 7 + q, 112, 4) for q in range(7)]
            t3 = gather3(row[4:])
            four = [
                jnp.concatenate(v, axis=0)
                for v in ((row[0], row[2]), (row[4], row[6]), (row[1], row[3]), (row[5], t3))
            ]
            pair.append((join(four[0], four[1]), join(four[2], four[3])))
        adjoint_put(xs_ref, k, pair[0], pair[1])
    for e in range(8):
        re, im = adjoint_child(xs_ref, wh_ref, wl_ref, e, kept(turn_ref, 8 * e, 4))
        for q, v in enumerate(quarters(re, im)):
            for p in range(2):
                start = (8 * p + e) * 16 + 4 * q
                out_ref[start : start + 4, :] = v[4 * p : 4 * p + 4]


def adjoint0(x_ref, wh_ref, wl_ref, turn_ref, out_ref, xs_ref, mid_ref):
    table = kept(turn_ref, 0, 4)
    for k in range(0, 8, 2):
        pair = [
            wide(x_ref, [(j >> 2) * 16 + c * 4 + (j & 3) for c in range(4)], 32)
            for j in (k, k + 1)
        ]
        adjoint_put(xs_ref, k, pair[0], pair[1])
    for e in range(8):
        re, im = adjoint_child(xs_ref, wh_ref, wl_ref, e, pick(table, e))
        ((c, s),) = kept(turn_ref, 8 + 2 * e, 1)
        for q, v in enumerate(quarters(re * c + im * s, im * c - re * s)):
            mid_ref[pl.ds(64 * q + e, 8, stride=8), :] = v
    pack(mid_ref, out_ref)


def call(kernel, name, out_shape, scratch, levels, *operands, space=pltpu.VMEM, room=16):
    several = isinstance(out_shape[0], tuple)
    shapes = [jax.ShapeDtypeStruct(v, F32) for v in (out_shape if several else (out_shape,))]
    place = pl.BlockSpec(memory_space=pltpu.VMEM)
    return pl.pallas_call(
        kernel,
        out_shape=shapes if several else shapes[0],
        in_specs=[pl.BlockSpec(memory_space=space)] * len(operands),
        out_specs=[place] * len(shapes) if several else place,
        scratch_shapes=scratch,
        compiler_params=pltpu.CompilerParams(vmem_limit_bytes=room * 2**20),
        cost_estimate=pl.CostEstimate(
            flops=levels * 10**9, bytes_accessed=2 * 10**6, transcendentals=0
        ),
        name=name,
    )(*operands)


def shards(forward_weights, adjoint_weights, medium):
    wh, wl = (jnp.asarray(v) for v in tables())
    medium = medium.reshape(1, 4)
    fscr = pltpu.VMEM((256, 8 * W), BF16)
    ascr = pltpu.VMEM((256, W), BF16)
    mid = pltpu.VMEM((256, 128), F32)
    tail = pltpu.VMEM((64, 128), F32)
    swap = functools.partial(lax.all_to_all, split_axis=0, concat_axis=0, tiled=True)

    def over(x, axis, count, rows):
        shape = x.shape
        return swap(x.reshape(count, -1, rows, 128), axis).reshape(shape)

    fw = forward_weights.reshape(64, 2 * Q)
    table = pltpu.VMEM((8 * W, W), BF16)
    own = [pltpu.VMEM((1, 4), F32), pltpu.VMEM((64, 2 * Q), F32), table, table]
    own.append(pltpu.SemaphoreType.DMA((2,)))
    f0 = call(
        forward0,
        "forward0",
        (256, 128),
        [fscr, tail] + own,
        1,
        medium,
        fw,
        space=pltpu.HBM,
        room=58,
    )
    f0 = over(f0, "sx", 16, 8)
    a2, turn1 = call(
        adjoint32,
        "adjoint32",
        ((224, 128), (512, W)),
        [ascr, mid, tail],
        2,
        medium,
        adjoint_weights,
        wh,
        wl,
    )
    both = call(forward1, "forward1", (448, 128), [fscr], 1, f0, wh, wl, a2, turn1)
    both = over(both, "sy", 32, 2)
    a1 = call(adjoint1, "adjoint1", (256, 128), [ascr], 1, both, wh, wl, turn1)
    a1 = over(a1, "sx", 16, 8)
    f3, turn0 = call(
        forward23, "forward23", ((64, 2 * Q), (192, W)), [fscr, mid], 2, medium, both, wh, wl
    )
    a0 = call(adjoint0, "adjoint0", (64, 2 * Q), [ascr, mid], 1, a1, wh, wl, turn0)
    return f3, a0.reshape(8, 8, 2 * Q)


def solution(mesh):
    return jax.shard_map(
        shards,
        mesh=mesh,
        in_specs=(P(("sy", "sx"), None, None), P(("sx", "sy"), None), P()),
        out_specs=(P(("sx", "sy"), None), P(None, ("sy", "sx"), None)),
        check_vma=False,
    )
```

```python
import functools
import math

import jax
import jax.numpy as jnp
import numpy as np
from jax import lax
from jax.experimental import pallas as pl
from jax.experimental.pallas import tpu as pltpu
from jax.sharding import PartitionSpec as P

ORDER = 6
Q = 216
W = 256
F32 = jnp.float32
BF16 = jnp.bfloat16
PATTERNS = (7, 6, 5, 4)
KORD = (7, 0, 6, 1, 5, 2, 4, 3)
CUT = 2 * Q - 384
SPILL = Q - 128


def cheb_points():
    return np.array([(1.0 - math.cos((2 * i + 1) * math.pi / (2 * ORDER))) / 2.0 for i in range(ORDER)])


def child_halves():
    nodes = cheb_points()
    halves = []
    for bit in range(2):
        matrix = np.zeros((ORDER, ORDER))
        for row in range(ORDER):
            where = (nodes[row] + bit) / 2.0
            for col in range(ORDER):
                value = 1.0
                for other in range(ORDER):
                    if other != col:
                        value *= (where - nodes[other]) / (nodes[col] - nodes[other])
                matrix[row, col] = value
        halves.append(matrix)
    return halves


def child_table():
    halves = child_halves()
    return np.stack(
        [np.kron(np.kron(halves[e // 4], halves[e // 2 % 2]), halves[e % 2]) for e in range(8)]
    )


def tables():
    table = np.zeros((8, W, W))
    table[:, :Q, :Q] = child_table() / math.sqrt(8.0)
    whole = table.reshape(8 * W, W).astype(np.float32)
    high = whole.astype(jnp.bfloat16)
    return high, (whole - high.astype(np.float32)).astype(jnp.bfloat16)


def turn_polynomials():
    x = (np.cos(np.pi * (np.arange(400) + 0.5) / 400) + 1.0) / 8.0
    f = np.sqrt(x)
    s = np.polynomial.chebyshev.Chebyshev.fit(x, np.sin(2 * np.pi * f) / f, 5, domain=[0, 0.25])
    c = np.polynomial.chebyshev.Chebyshev.fit(x, np.cos(2 * np.pi * f), 6, domain=[0, 0.25])
    return [
        [float(v) for v in p.convert(kind=np.polynomial.Polynomial).coef] for p in (s, c)
    ]


SIN, COS = turn_polynomials()


def horner(coefs, z):
    value = jnp.full_like(z, coefs[-1])
    for c in coefs[-2::-1]:
        value = value * z + c
    return value


def cis(turns):
    f = turns - jnp.round(turns)
    z = f * f
    return horner(COS, z), f * horner(SIN, z)


def digit_coords(index, digits):
    out = []
    for bit in (2, 1, 0):
        value = None
        for d in range(digits):
            part = (index >> (3 * d + bit)) & 1
            part = part << d if d else part
            value = part if value is None else value + part
        out.append(value)
    return out


def as_f32(values):
    return [v.astype(F32) for v in values]


def rows8():
    return lax.broadcasted_iota(jnp.int32, (8, W), 0)


def point_digits(t):
    i = (t * 7282) >> 18
    ij = (t * 10923) >> 16
    return i, ij - 6 * i, t - 6 * ij


def table_factors():
    lane = lax.broadcasted_iota(jnp.int32, (W, 128), 1)
    wanted = jnp.where(lane < 24, lane & 7, 8)
    picks = [
        jnp.where(n == wanted, 1.0, 0.0).astype(BF16)
        for n in point_digits(lax.broadcasted_iota(jnp.int32, (W, 128), 0))
    ]
    digits = point_digits(lax.broadcasted_iota(jnp.int32, (8, W), 1))
    row = rows8()
    factors = [[], [], []]
    for half in child_halves():
        rest = half / math.sqrt(2.0)
        pieces = [[], [], []]
        for _ in range(3):
            piece = rest.astype(jnp.bfloat16).astype(np.float64)
            rest = rest - piece
            columns = []
            for i in range(ORDER):
                column = jnp.zeros((8, W), F32)
                for m in range(ORDER):
                    column = jnp.where(row == m, float(piece[m, i]), column)
                columns.append(column)
            for d in range(3):
                value = jnp.zeros((8, W), F32)
                for i in range(ORDER):
                    value = jnp.where(digits[d] == i, columns[i], value)
                pieces[d].append(value)
        for d in range(3):
            spread_rows = jnp.concatenate(pieces[d] + [jnp.zeros((104, W), F32)], axis=0)
            factors[d].append(
                jnp.dot(picks[d], spread_rows.astype(BF16), preferred_element_type=F32)
            )
    return factors


def built_product(factors, xs_ref):
    total = None
    for yz in range(4):
        part = factors[1][yz >> 1] * factors[2][yz & 1]
        for x in range(2):
            whole = factors[0][x] * part
            high = whole.astype(BF16)
            low = (whole - high.astype(F32)).astype(BF16)
            cols = slice((4 * x + yz) * W, (4 * x + yz + 1) * W)
            one = product(xs_ref[:, cols], xs_ref[0:128, cols], high, low, 0)
            total = one if total is None else total + one
    return total


def grid_points():
    t = lax.broadcasted_iota(jnp.int32, (8, W), 1)
    nodes = [float(v) for v in cheb_points()]
    out = []
    for n in point_digits(t):
        value = jnp.full((8, W), nodes[5], F32)
        for m in range(4, -1, -1):
            value = jnp.where(n == m, nodes[m], value)
        out.append(value)
    return out


def travel_rays(corner, side, grid, med):
    p = [side * (corner[d] + grid[d]) for d in range(3)]
    r = jnp.sqrt(p[0] * p[0] + p[1] * p[1] + p[2] * p[2])
    return r, [p[d] + med[d + 1] * r for d in range(3)]


def patterns(level, rays):
    step = 1.0 / 2 ** (level + 3)
    x, y, z = (step * v for v in rays)
    a, b = x + y, x - y
    return [cis(a + z), cis(a - z), cis(b + z), cis(b - z)]


def pick(table, row):
    return [(c[row : row + 1, :], s[row : row + 1, :]) for c, s in table]


def split16(first, second):
    whole = jnp.concatenate([first, second], axis=0)
    high = whole.astype(BF16)
    return high, (whole - high.astype(F32)).astype(BF16)


def forward_put(xs_ref, e, re, im, turn):
    cols = slice(e * W, (e + 1) * W)
    for s, (c, sn) in enumerate(turn):
        a, b, d, g = re * c, im * sn, im * c, re * sn
        for base, one, two in ((0, a - b, a + b), (64, d + g, d - g)):
            high, low = split16(one, two)
            row = base + 16 * s
            xs_ref[row : row + 16, cols] = high
            xs_ref[128 + row : 144 + row, cols] = low


def product(x, xh, wh, wl, side):
    dot = functools.partial(
        lax.dot_general, dimension_numbers=(((1,), (side,)), ((), ())), preferred_element_type=F32
    )
    both = dot(x, wh)
    return both[:128] + both[128:] + dot(xh, wl)


def forward_product(xs_ref, wh_ref, wl_ref):
    return product(xs_ref[...], xs_ref[0:128, :], wh_ref[...], wl_ref[...], 0)


def adjoint_put(xs_ref, k, first, second):
    for base, one, two in ((0, first[0], second[0]), (64, first[1], second[1])):
        high, low = split16(one, two)
        row = base + 8 * k
        xs_ref[row : row + 16, :] = high
        xs_ref[128 + row : 144 + row, :] = low


def adjoint_child(xs_ref, wh_ref, wl_ref, e, turn):
    cols = slice(e * W, (e + 1) * W)
    y = product(xs_ref[...], xs_ref[0:128, :], wh_ref[cols, :], wl_ref[cols, :], 1)
    re = im = None
    for k, (c, sn) in zip(PATTERNS, turn):
        o = 7 - k
        kr, ki = y[8 * k : 8 * k + 8], y[64 + 8 * k : 72 + 8 * k]
        br, bi = y[8 * o : 8 * o + 8], y[64 + 8 * o : 72 + 8 * o]
        one = c * (kr + br) + sn * (ki - bi)
        two = c * (ki + bi) - sn * (kr - br)
        re, im = (one, two) if re is None else (re + one, im + two)
    return re, im


def quarters(re, im):
    return re[:, :128], re[:, 128:], im[:, :128], im[:, 128:]


def join(a, b):
    return jnp.concatenate([a, b], axis=1)


def unpack(x_ref, tail_ref):
    tail_ref[...] = jnp.zeros_like(tail_ref)
    tail_ref[:, 0:CUT] = x_ref[:, 384 : 2 * Q]
    lane = lax.broadcasted_iota(jnp.int32, (64, 128), 1)
    x0, x1, x2, x3 = x_ref[:, 0:128], x_ref[:, 128:256], x_ref[:, 256:384], tail_ref[...]
    shift = 128 - SPILL
    r1, r2, r3 = (pltpu.roll(v, shift, 1) for v in (x1, x2, x3))
    re = join(x0, jnp.where(lane < SPILL, x1, 0.0))
    im = join(
        jnp.where(lane < shift, r1, r2),
        jnp.where(lane < shift, r2, jnp.where(lane < SPILL, r3, 0.0)),
    )
    return re, im


def pack(parts, out_ref):
    r0, r1, i0, i1 = (parts[64 * c : 64 * c + 64, :] for c in range(4))
    lane = lax.broadcasted_iota(jnp.int32, (64, 128), 1)
    s0, s1 = pltpu.roll(i0, SPILL, 1), pltpu.roll(i1, SPILL, 1)
    out_ref[:, 0:128] = r0
    out_ref[:, 128:256] = jnp.where(lane < SPILL, r1, s0)
    out_ref[:, 256:384] = jnp.where(lane < SPILL, s0, s1)
    out_ref[:, 384 : 2 * Q] = s1[:, 0:CUT]


def lanes(shape):
    return lax.broadcasted_iota(jnp.int32, shape, 1)


def spread(t3, rows):
    own = lanes(rows[0].shape) < SPILL
    return [
        jnp.where(own, row, pltpu.roll(t, shift, 1))
        for row, t, shift in zip(rows, t3, (SPILL, SPILL - 40, SPILL - 80))
    ]


def gather3(rows):
    a, b, c = (pltpu.roll(v, s, 1) for v, s in zip(rows, (40, 80, 120)))
    lane = lanes(a.shape)
    return jnp.where(lane < 40, a, jnp.where(lane < 80, b, c))


def medium_of(med_ref):
    return [jnp.broadcast_to(med_ref[0:1, i : i + 1], (8, W)) for i in range(4)]


def own_source(extra_rows):
    own = lax.axis_index("sy") * 16 + lax.axis_index("sx")
    high = digit_coords(own, 3)
    low = digit_coords(extra_rows, 1)
    return as_f32([low[d] + 2 * high[d] for d in range(3)])


def root_turn(med, corner, rays0):
    r, rays = rays0
    centre = [(v + 0.5) * 0.5 for v in corner]
    travel = med[0] * r
    return cis(travel + centre[0] * rays[0] + centre[1] * rays[1] + centre[2] * rays[2])


def end_turn(med, block, across, grid):
    own = lax.axis_index("sx") * 32 + lax.axis_index("sy")
    high = digit_coords(own, 3)
    row = digit_coords(rows8(), 1)
    fixed = digit_coords(block, 1)
    wr, wf = (1, 2) if across else (2, 1)
    centre = [
        ((4 * high[d] + wf * fixed[d] + wr * row[d]).astype(F32) + 0.5) * (1.0 / 32.0)
        for d in range(3)
    ]
    p = [8.0 * grid[d] for d in range(3)]
    r = jnp.sqrt(p[0] * p[0] + p[1] * p[1] + p[2] * p[2])
    u = med[0] * r
    for d in range(3):
        u = u + centre[d] * (p[d] + med[d + 1] * r)
    return cis(u)


def level_patterns(level, corner, side, grid, med):
    return patterns(level, travel_rays(corner, side, grid, med)[1])


def level1_tables(grid, med):
    high = digit_coords(lax.axis_index("sy") * 2, 2)
    first = digit_coords(rows8(), 1)
    out = []
    for half in range(2):
        mid = digit_coords(lax.axis_index("sy") * 2 + half, 2)
        corner = as_f32([first[d] + 2 * mid[d] for d in range(3)])
        out.append(level_patterns(1, corner, 1.0, grid, med))
    return out


def level1_turn(both, e):
    upper = rows8() < 4
    return [
        (
            jnp.where(upper, c0[e : e + 1, :], c1[e : e + 1, :]),
            jnp.where(upper, s0[e : e + 1, :], s1[e : e + 1, :]),
        )
        for (c0, s0), (c1, s1) in zip(*both)
    ]


def level2_turn(e, grid, med):
    parent = digit_coords(rows8(), 1)
    child = digit_coords(e, 1)
    corner = as_f32([2 * parent[d] + child[d] for d in range(3)])
    return level_patterns(2, corner, 2.0, grid, med)


def level3_table(grid, med):
    return level_patterns(3, as_f32(digit_coords(rows8(), 1)), 4.0, grid, med)


def keep(ref, slot, turn):
    for i, value in enumerate(v for pair in turn for v in pair):
        ref[8 * (slot + i) : 8 * (slot + i) + 8, :] = value


def kept(ref, slot, count):
    rows = [ref[8 * (slot + i) : 8 * (slot + i) + 8, :] for i in range(2 * count)]
    return list(zip(rows[::2], rows[1::2]))


def rows_of(ref, start, stride, count=8):
    return ref[pl.ds(start, count, stride=stride), :]


def wide(ref, start, stride):
    return join(rows_of(ref, start[0], stride), rows_of(ref, start[1], stride)), join(
        rows_of(ref, start[2], stride), rows_of(ref, start[3], stride)
    )


def forward0(med_hbm, x_hbm, out_ref, xs_ref, tail_ref, med_ref, x_ref, sems):
    copies = [
        pltpu.make_async_copy(med_hbm, med_ref, sems.at[0]),
        pltpu.make_async_copy(x_hbm, x_ref, sems.at[1]),
    ]
    for copy in copies:
        copy.start()
    factors = table_factors()
    copies[0].wait()
    med, grid = medium_of(med_ref), grid_points()
    r, rays = travel_rays(own_source(rows8()), 0.5, grid, med)
    table = patterns(0, rays)
    target = as_f32(digit_coords(rows8(), 1))
    turns = []
    for e in range(8):
        one = slice(e, e + 1)
        turns.append(root_turn(med, target, (r[one], [v[one] for v in rays])))
    copies[1].wait()
    re, im = unpack(x_ref, tail_ref)
    for e in range(8):
        c, s = turns[e]
        xr, xi = re[8 * e : 8 * e + 8], im[8 * e : 8 * e + 8]
        forward_put(xs_ref, e, xr * c - xi * s, xr * s + xi * c, pick(table, e))
    y = built_product(factors, xs_ref)
    for pos, k in enumerate(KORD):
        four = quarters(y[8 * pos : 8 * pos + 8], y[64 + 8 * pos : 72 + 8 * pos])
        for c, v in enumerate(four):
            out_ref[pl.ds((k >> 2) * 16 + c * 4 + (k & 3), 8, stride=32), :] = v


def forward1(x_ref, wh_ref, wl_ref, other_ref, turn_ref, out_ref, xs_ref):
    for q in range(7):
        for group in range(0, 32, 8):
            out_ref[pl.ds(group * 14 + 7 + q, 8, stride=14), :] = other_ref[
                q * 32 + group : q * 32 + group + 8, :
            ]
    upper = lax.broadcasted_iota(jnp.int32, (8, 128), 0) < 4
    for e in range(8):
        halves = []
        for part in range(2):
            t0 = x_ref[e * 16 + 8 * part : e * 16 + 8 * part + 8, :]
            t1 = x_ref[128 + e * 16 + 8 * part : 128 + e * 16 + 8 * part + 8, :]
            halves.append(
                join(
                    jnp.where(upper, t0, pltpu.roll(t1, 4, 0)),
                    jnp.where(upper, pltpu.roll(t0, 4, 0), t1),
                )
            )
        forward_put(xs_ref, e, halves[0], halves[1], kept(turn_ref, 8 * e, 4))
    y = forward_product(xs_ref, wh_ref, wl_ref)
    for pos, k in enumerate(KORD):
        r0, r1, i0, i1 = quarters(y[8 * pos : 8 * pos + 8], y[64 + 8 * pos : 72 + 8 * pos])
        last = pltpu.roll(i1, 4, 0)
        u4, u5, u6 = spread((last, last, i1), (r1, i1, r1))
        low, high = slice(0, 4), slice(4, 8)
        rows = (r0[low], i0[low], r0[high], i0[high], u4[low], u5[low], u6[high])
        for q, v in enumerate(rows):
            out_ref[pl.ds(k * 14 + q, 4, stride=112), :] = v


def forward23(med_ref, x_ref, wh_ref, wl_ref, out_ref, turn_ref, xs_ref, mid_ref):
    med, grid = medium_of(med_ref), grid_points()
    for m in range(4):
        row = [rows_of(x_ref, m * 14 + q, 56) for q in range(7)]
        pair = (
            (join(row[0], row[4]), join(row[1], row[5])),
            (join(row[2], row[6]), join(row[3], gather3(row[4:]))),
        )
        for e, (re, im) in zip((2 * m, 2 * m + 1), pair):
            forward_put(xs_ref, e, re, im, level2_turn(e, grid, med))
    y = forward_product(xs_ref, wh_ref, wl_ref)
    for pos, k in enumerate(KORD):
        four = quarters(y[8 * pos : 8 * pos + 8], y[64 + 8 * pos : 72 + 8 * pos])
        for c, v in enumerate(four):
            mid_ref[64 * c + 8 * k : 64 * c + 8 * k + 8, :] = v
    table = level3_table(grid, med)
    for e in range(8):
        re, im = wide(mid_ref, [64 * c + e for c in range(4)], 8)
        forward_put(xs_ref, e, re, im, pick(table, e))
    y = forward_product(xs_ref, wh_ref, wl_ref)
    for pos, k in enumerate(KORD):
        c, s = end_turn(med, k, False, grid)
        re, im = y[8 * pos : 8 * pos + 8], y[64 + 8 * pos : 72 + 8 * pos]
        four = quarters(re * c + im * s, im * c - re * s)
        for q, v in enumerate(four):
            mid_ref[pl.ds(64 * q + k, 8, stride=8), :] = v
    pack(mid_ref, out_ref)
    r, rays = travel_rays(own_source(rows8()), 0.5, grid, med)
    keep(turn_ref, 0, patterns(0, rays))
    target = as_f32(digit_coords(rows8(), 1))
    for e in range(8):
        one = slice(e, e + 1)
        keep(turn_ref, 8 + 2 * e, [root_turn(med, target, (r[one], [v[one] for v in rays]))])


def adjoint32(med_ref, x_ref, wh_ref, wl_ref, out_ref, turn_ref, xs_ref, mid_ref, tail_ref):
    med, grid = medium_of(med_ref), grid_points()
    re, im = unpack(x_ref, tail_ref)
    for k in range(8):
        c, s = end_turn(med, k, True, grid)
        xr, xi = re[8 * k : 8 * k + 8], im[8 * k : 8 * k + 8]
        for q, v in enumerate(quarters(xr * c - xi * s, xr * s + xi * c)):
            mid_ref[64 * q + 8 * k : 64 * q + 8 * k + 8, :] = v
    for k in range(0, 8, 2):
        adjoint_put(
            xs_ref,
            k,
            wide(mid_ref, [64 * c + k for c in range(4)], 8),
            wide(mid_ref, [64 * c + k + 1 for c in range(4)], 8),
        )
    table = level3_table(grid, med)
    for e in range(8):
        re, im = adjoint_child(xs_ref, wh_ref, wl_ref, e, pick(table, e))
        for q, v in enumerate(quarters(re, im)):
            mid_ref[pl.ds(64 * q + e, 8, stride=8), :] = v
    for k in range(0, 8, 2):
        pair = []
        for j in (k, k + 1):
            r0, r1, i0, i1 = (mid_ref[64 * c + 8 * j : 64 * c + 8 * j + 8, :] for c in range(4))
            pair.append((join(r0, r1), join(i0, i1)))
        adjoint_put(xs_ref, k, pair[0], pair[1])
    for m in range(4):
        first, second = (
            quarters(*adjoint_child(xs_ref, wh_ref, wl_ref, e, level2_turn(e, grid, med)))
            for e in (2 * m, 2 * m + 1)
        )
        tails = spread((second[3],) * 3, (first[1], first[3], second[1]))
        for q, v in enumerate((first[0], first[2], second[0], second[2], *tails)):
            out_ref[pl.ds(q * 32 + m, 8, stride=4), :] = v
    both = level1_tables(grid, med)
    for e in range(8):
        keep(turn_ref, 8 * e, level1_turn(both, e))


def adjoint1(x_ref, wh_ref, wl_ref, turn_ref, out_ref, xs_ref):
    for k in range(0, 8, 2):
        pair = []
        for j in (k, k + 1):
            row = [rows_of(x_ref, j * 14 + 7 + q, 112, 4) for q in range(7)]
            t3 = gather3(row[4:])
            four = [
                jnp.concatenate(v, axis=0)
                for v in ((row[0], row[2]), (row[4], row[6]), (row[1], row[3]), (row[5], t3))
            ]
            pair.append((join(four[0], four[1]), join(four[2], four[3])))
        adjoint_put(xs_ref, k, pair[0], pair[1])
    for e in range(8):
        re, im = adjoint_child(xs_ref, wh_ref, wl_ref, e, kept(turn_ref, 8 * e, 4))
        for q, v in enumerate(quarters(re, im)):
            for p in range(2):
                start = (8 * p + e) * 16 + 4 * q
                out_ref[start : start + 4, :] = v[4 * p : 4 * p + 4]


def adjoint0(x_ref, wh_ref, wl_ref, turn_ref, out_ref, xs_ref, mid_ref):
    table = kept(turn_ref, 0, 4)
    for k in range(0, 8, 2):
        pair = [
            wide(x_ref, [(j >> 2) * 16 + c * 4 + (j & 3) for c in range(4)], 32)
            for j in (k, k + 1)
        ]
        adjoint_put(xs_ref, k, pair[0], pair[1])
    for e in range(8):
        re, im = adjoint_child(xs_ref, wh_ref, wl_ref, e, pick(table, e))
        ((c, s),) = kept(turn_ref, 8 + 2 * e, 1)
        for q, v in enumerate(quarters(re * c + im * s, im * c - re * s)):
            mid_ref[pl.ds(64 * q + e, 8, stride=8), :] = v
    pack(mid_ref, out_ref)


def call(kernel, name, out_shape, scratch, levels, *operands, space=pltpu.VMEM, room=16):
    several = isinstance(out_shape[0], tuple)
    shapes = [jax.ShapeDtypeStruct(v, F32) for v in (out_shape if several else (out_shape,))]
    place = pl.BlockSpec(memory_space=pltpu.VMEM)
    return pl.pallas_call(
        kernel,
        out_shape=shapes if several else shapes[0],
        in_specs=[pl.BlockSpec(memory_space=space)] * len(operands),
        out_specs=[place] * len(shapes) if several else place,
        scratch_shapes=scratch,
        compiler_params=pltpu.CompilerParams(vmem_limit_bytes=room * 2**20),
        cost_estimate=pl.CostEstimate(
            flops=levels * 10**9, bytes_accessed=2 * 10**6, transcendentals=0
        ),
        name=name,
    )(*operands)


def shards(forward_weights, adjoint_weights, medium):
    wh, wl = (jnp.asarray(v) for v in tables())
    medium = medium.reshape(1, 4)
    fscr = pltpu.VMEM((256, 8 * W), BF16)
    ascr = pltpu.VMEM((256, W), BF16)
    mid = pltpu.VMEM((256, 128), F32)
    tail = pltpu.VMEM((64, 128), F32)
    swap = functools.partial(lax.all_to_all, split_axis=0, concat_axis=0, tiled=True)

    def over(x, axis, count, rows):
        shape = x.shape
        return swap(x.reshape(count, -1, rows, 128), axis).reshape(shape)

    fw = forward_weights.reshape(64, 2 * Q)
    own = [pltpu.VMEM((1, 4), F32), pltpu.VMEM((64, 2 * Q), F32)]
    own.append(pltpu.SemaphoreType.DMA((2,)))
    f0 = call(
        forward0,
        "forward0",
        (256, 128),
        [fscr, tail] + own,
        1,
        medium,
        fw,
        space=pltpu.HBM,
        room=58,
    )
    f0 = over(f0, "sx", 16, 8)
    a2, turn1 = call(
        adjoint32,
        "adjoint32",
        ((224, 128), (512, W)),
        [ascr, mid, tail],
        2,
        medium,
        adjoint_weights,
        wh,
        wl,
    )
    both = call(forward1, "forward1", (448, 128), [fscr], 1, f0, wh, wl, a2, turn1)
    both = over(both, "sy", 32, 2)
    a1 = call(adjoint1, "adjoint1", (256, 128), [ascr], 1, both, wh, wl, turn1)
    a1 = over(a1, "sx", 16, 8)
    f3, turn0 = call(
        forward23, "forward23", ((64, 2 * Q), (192, W)), [fscr, mid], 2, medium, both, wh, wl
    )
    a0 = call(adjoint0, "adjoint0", (64, 2 * Q), [ascr, mid], 1, a1, wh, wl, turn0)
    return f3, a0.reshape(8, 8, 2 * Q)


def solution(mesh):
    return jax.shard_map(
        shards,
        mesh=mesh,
        in_specs=(P(("sy", "sx"), None, None), P(("sx", "sy"), None), P()),
        out_specs=(P(("sx", "sy"), None), P(None, ("sy", "sx"), None)),
        check_vma=False,
    )
```
